256 devices in a mesh: island: 16 (over z_lo, y), fsdp: 16 (over z_hi, x, core).
Axes of the slice: x: 4, y: 4, z: 8 (z_hi: 2, z_lo: 4; z = z_hi * 4 + z_lo), core: 2. Of those that a mesh axis runs over, the one named last changes fastest.
Arguments:
- tokens_in: bfloat16 [16, 2, 4096, 8192], P('island', None, 'fsdp'), may hold values from -6 to 6
- norm_gain: float32 [8192], replicated, may hold values from 0.1 to 1.9
- local_weights: float32 [16, 8192, 512], P('island', 'fsdp'), may hold values from -0.0625 to 0.0625
- cotangent: bfloat16 [16, 2, 4096, 512], P('island', None, 'fsdp'), may hold values from -6 to 6
- delta_levels: bfloat16 [16, 8192, 512], P('island', 'fsdp'), may hold values from -127 to 127, as said below
- block_scales: float32 [16, 8192, 4], P('island', 'fsdp'), may hold values from 5.5242715e-05 to 0.0002762136
- outer_weights_in: float32 [8192, 512], P('fsdp'), may hold values from -0.0625 to 0.0625
- momentum_in: float32 [8192, 512], P('fsdp'), may hold values from -0.03314563 to 0.03314563
Outputs:
- keys: bfloat16 [16, 2, 4096, 512], P('island', None, 'fsdp')
- merged: float32 [16, 8192, 512], P('island', 'fsdp')
- outer_weights: float32 [8192, 512], P('fsdp')
- outer_momentum: float32 [8192, 512], P('fsdp')
The draws below stay inside these ranges and needn't reach their ends.
Inputs may be any that keep to these rules, and one draw needn't show every extreme that they name: `delta_levels`: whole numbers.
All inputs are finite; a program needn't handle non-finite values.
Results may differ from the reference program's by a relative error of at most 0.012.
Values may be sent and summed in bfloat16 or wider, within the bound.
A program may use at most 128 MiB of HBM per device.

```python
import math
import jax
import jax.numpy as jnp
from jax import lax

D = 8192
KV = 512
BLOCK = 128
MICRO = 2
TOKENS = 4096
ISLANDS = 16


def draw_delta_levels(key, part):
    key = jax.random.fold_in(key, 11)
    levels = jax.random.randint(key, (ISLANDS, D, KV), -127, 128)
    levels = levels.at[:, 0, 0].set(127)
    levels = levels.at[:, 0, 1].set(-127)
    return levels.astype(jnp.bfloat16)


def raised(values, own_key, source, target, parts, factor):
    owner, partner = [(jnp.arange(values.shape[axis_at]) // (values.shape[axis_at] // parts)).reshape([-1 if axis == axis_at else 1 for axis in range(values.ndim)]) for axis_at in (source, target)]
    chosen = jax.random.permutation(own_key, parts)[partner]
    strong = (owner == chosen) | (owner == (partner + parts // 2) % parts)
    return jnp.where(strong, factor * values, values)


def shard_levels(stream_key, extent, split, low, top_value):
    def one(dim, parts):
        draws = jax.random.uniform(jax.random.fold_in(jax.random.fold_in(stream_key, 6), dim), (parts,), jnp.float32, low / len(split), top_value / len(split))
        return jnp.repeat(jnp.exp(draws), extent[dim] // parts).reshape((-1,) + (1,) * (len(extent) - dim - 1))

    loudness = one(*split[0])
    for cut in split[1:]:
        loudness = loudness * one(*cut)
    return loudness


def gaussian(stream_key, shape, deviation, bound, pieces=(), held_as=jnp.bfloat16):
    array = jax.random.normal(stream_key, shape, jnp.float32) * deviation
    if len(pieces) > 0:
        array = shard_levels(stream_key, shape, pieces, -0.22, 0.18) * array
    return jnp.clip(array, min=-bound, max=bound).astype(held_as)


def heavy_noise(own_key, extent, width, limit, shards, heavy, held_as=jnp.bfloat16):
    array = width * jax.random.normal(own_key, extent, jnp.float32)
    if shards:
        array = array * shard_levels(own_key, extent, shards, -0.22, 0.18)
    return jnp.clip(raised(array, jax.random.fold_in(own_key, 3), *heavy), -limit, limit).astype(held_as)


def setup_inputs(seed: int = 0) -> dict:
    streams_of = jax.random.split(jax.random.key(seed), 9)
    tokens_in = heavy_noise(streams_of[0], (ISLANDS, MICRO, TOKENS, D), 1.0, 6.0, ((0, 16), (2, 16)), (2, 3, 16, 2.0))
    norm_gain = jnp.clip(1.0 + 0.18 * jax.random.normal(streams_of[1], (D,), jnp.float32), 0.1, 1.9)
    local_weights = gaussian(streams_of[2], (ISLANDS, D, KV), D ** -0.5, 0.0625, ((0, 16), (1, 16)), jnp.float32)
    cotangent = gaussian(streams_of[3], (ISLANDS, MICRO, TOKENS, KV), 1.0, 6.0, ((0, 16), (2, 16)))
    delta_levels = draw_delta_levels(jax.random.fold_in(streams_of[8], 71), 0)
    block_scales = jnp.clip(jnp.exp(math.log(0.0002762136) - 1.609438 * jax.random.uniform(streams_of[5], (ISLANDS, D, KV // BLOCK), jnp.float32) ** shard_levels(streams_of[5], (ISLANDS, D, KV // BLOCK), ((0, 16), (1, 16)), -0.2, 0.2)), 5.5242715461645275e-05, 0.0002762136)
    outer_weights_in = gaussian(streams_of[6], (D, KV), D ** -0.5, 0.0625, ((0, 16),), jnp.float32)
    momentum_in = gaussian(streams_of[7], (D, KV), (0.5 / D ** 0.5), 0.03314563, ((0, 16),), jnp.float32)
    return {"tokens_in": tokens_in, "norm_gain": norm_gain, "local_weights": local_weights, "cotangent": cotangent, "delta_levels": delta_levels, "block_scales": block_scales, "outer_weights_in": outer_weights_in, "momentum_in": momentum_in}


norm_eps = 1e-05
inner_rate = 0.3
outer_rate = 0.7
keep_rate = 0.9
mix_share = 0.5

def reference(tokens_in, norm_gain, local_weights, cotangent, delta_levels, block_scales, outer_weights_in, momentum_in):
    scale_root = math.sqrt(D)
    step_scale = 1.0 / math.sqrt(MICRO * TOKENS)

    def island(packed):
        activations, weights, tangent = packed
        widened = activations.astype(jnp.float32)
        spread = lax.optimization_barrier(jnp.mean(widened * widened, axis=-1, keepdims=True))
        normed = (widened * lax.rsqrt(spread + norm_eps) * norm_gain).astype(jnp.bfloat16)
        token_rows = normed.reshape(MICRO * TOKENS, D)
        compute_weights = weights.astype(jnp.bfloat16)
        projected = jnp.dot(token_rows, compute_weights, preferred_element_type=jnp.float32)
        key_block = projected.astype(jnp.bfloat16).reshape(MICRO, TOKENS, KV)
        gradient = jnp.dot(token_rows.T, tangent.reshape(MICRO * TOKENS, KV), preferred_element_type=jnp.float32) / scale_root
        inner_weights = weights - inner_rate * step_scale * gradient
        return (key_block, inner_weights)
    keys, inner_all = lax.map(island, (tokens_in, local_weights, cotangent))
    dequantized = delta_levels.astype(jnp.float32) * jnp.repeat(block_scales, BLOCK, axis=2)
    mean_delta = lax.optimization_barrier(jnp.sum(dequantized, axis=0)) / ISLANDS
    outer_momentum = keep_rate * momentum_in + mean_delta
    outer_weights = outer_weights_in - outer_rate * (mean_delta + keep_rate * outer_momentum)
    merged = mix_share * inner_all + (1.0 - mix_share) * outer_weights[None]
    return (keys, merged, outer_weights, outer_momentum)
```

```python
import functools
import math

import jax
import jax.numpy as jnp
from jax import lax
from jax.experimental import pallas as pl
from jax.experimental.pallas import tpu as pltpu
from jax.sharding import PartitionSpec as P

BLOCK = 128
NX = 4
NY = 4
NZ = 4
ROWS = 512
KV = 512
D = 8192
HALF = 256
QUARTER = 128
CHUNK = 64

norm_eps = 1e-05
inner_rate = 0.3
outer_rate = 0.7
keep_rate = 0.9
mix_share = 0.5

MESH = pl.DeviceIdType.MESH
f32 = jnp.float32
bf16 = jnp.bfloat16


def kernel(
    step_scale,
    tok_hbm,
    gain,
    w_hbm,
    cot_hbm,
    lev_hbm,
    scales,
    keys_out,
    inner_out,
    sum_out,
    tok,
    wf,
    cot,
    lev,
    wg,
    acc,
    p_out,
    p_in,
    q,
    r_a,
    r_b,
    from_m,
    from_p,
    z_out,
    z_in,
    y_in,
    zl_in,
    load_sem,
    send_sem,
    recv_sem,
):
    f = lax.axis_index("fsdp")
    i = lax.axis_index("island")
    zh, x, c = f // 8, (f // 2) % NX, f % 2
    zl, y = i // NY, i % NY

    def fs(dz, dx, dc):
        return ((zh + dz) % 2) * 8 + ((x + dx) % NX) * 2 + (c + dc) % 2

    def to_fsdp(dz, dx, dc):
        return {"fsdp": fs(dz, dx, dc), "island": i}

    def to_island(dzl, dy):
        return {"fsdp": f, "island": ((zl + dzl) % NZ) * NY + (y + dy) % NY}

    right, left = to_fsdp(0, 1, 0), to_fsdp(0, NX - 1, 0)
    across, other = to_fsdp(1, 0, 0), to_fsdp(0, 0, 1)

    started = []

    def remote(k, src, dst, device):
        return pltpu.make_async_remote_copy(
            src_ref=src,
            dst_ref=dst,
            send_sem=send_sem.at[k],
            recv_sem=recv_sem.at[k],
            device_id=device,
            device_id_type=MESH,
        )

    counter = [0]

    def role(src, dst, device):
        copy = remote(counter[0], src, dst, device)
        counter[0] += 1
        started.append(copy)
        return copy

    load_w = pltpu.make_async_copy(w_hbm, wf, load_sem.at[0])
    load_w.start()
    load_lev = pltpu.make_async_copy(lev_hbm, lev, load_sem.at[1])
    load_lev.start()
    loads = []
    for n in range(ROWS // CHUNK):
        rows = pl.ds(n * CHUNK, CHUNK)
        load = pltpu.make_async_copy(tok_hbm.at[rows], tok.at[rows], load_sem.at[3 + n])
        load.start()
        loads.append(load)
    load_cot = pltpu.make_async_copy(cot_hbm, cot, load_sem.at[2])
    load_cot.start()

    barrier = pltpu.get_barrier_semaphore()
    peers = [right, left, across, other]
    peers += [to_island(0, d) for d in (1, 2, 3)] + [to_island(d, 0) for d in (1, 2, 3)]
    for peer in peers:
        pl.semaphore_signal(barrier, inc=1, device_id=peer, device_id_type=MESH)
    load_w.wait()
    wg[0, 0, 0] = wf[...].astype(bf16)
    pl.semaphore_wait(barrier, len(peers))

    def quarter(n):
        return pl.ds(n * QUARTER, QUARTER)

    ag_right, ag_left, ag_relay, ag_other = {}, {}, {}, {}
    for zz in range(2):
        for n in (0, 1, 2, 3):
            rows = quarter(n)
            ag_right[zz, n] = role(wg.at[zz, 0, 0, rows], wg.at[zz, 3, 0, rows], right)
        for n in (1, 0, 3, 2):
            rows = quarter(n)
            ag_left[zz, n] = role(wg.at[zz, 0, 0, rows], wg.at[zz, 1, 0, rows], left)
        for n in (0, 2):
            rows = quarter(n)
            ag_relay[zz, n] = role(wg.at[zz, 3, 0, rows], wg.at[zz, 2, 0, rows], right)
        for n in (1, 3):
            rows = quarter(n)
            ag_relay[zz, n] = role(wg.at[zz, 1, 0, rows], wg.at[zz, 2, 0, rows], left)
        for dx in range(4):
            ag_other[zz, dx] = role(wg.at[zz, dx, 0], wg.at[zz, dx, 1], other)
    ag_z = [role(wg.at[0, 0, 0, quarter(n)], wg.at[1, 0, 0, quarter(n)], across) for n in range(4)]

    low, high = pl.ds(0, HALF), pl.ds(HALF, HALF)
    opp_left, opp_right, dir_right, dir_left, sum_right, sum_left = {}, {}, {}, {}, {}, {}
    for zz in range(2):
        opp_left[zz] = role(q.at[zz, 2, low], r_a.at[zz], left)
        opp_right[zz] = role(q.at[zz, 2, high], r_b.at[zz], right)
        dir_right[zz] = role(q.at[zz, 1, low], from_m.at[zz, low], right)
        dir_left[zz] = role(q.at[zz, 3, high], from_p.at[zz, high], left)
        for n in range(2):
            rows = pl.ds(HALF + n * QUARTER, QUARTER)
            sum_right[zz, n] = role(q.at[zz, 1, rows], from_m.at[zz, rows], right)
            rows = pl.ds(n * QUARTER, QUARTER)
            sum_left[zz, n] = role(q.at[zz, 3, rows], from_p.at[zz, rows], left)
    z_send = [role(z_out.at[quarter(n)], z_in.at[quarter(n)], across) for n in range(4)]

    y_part = []
    for d in (1, 2, 3):
        rows = pl.ds(pl.multiple_of(((y + d) % NY) * QUARTER, QUARTER), QUARTER)
        y_part.append(role(lev.at[rows], y_in.at[d - 1], to_island(0, d)))
    zl_part = [role(zl_in.at[zl], zl_in.at[zl], to_island(d, 0)) for d in (1, 2, 3)]
    mine = pl.ds(pl.multiple_of(y * QUARTER, QUARTER), QUARTER)
    y_sum = [role(sum_out.at[mine], sum_out.at[mine], to_island(0, d)) for d in (1, 2, 3)]

    base = counter[0]

    def pair(zz, dx):
        return remote(base + zz * 4 + dx, p_out.at[zz, dx], p_in.at[zz, dx], other)

    for n in range(2):
        for m in range(2):
            ag_right[0, 2 * n + m].start()
            ag_left[0, 2 * n + 1 - m].start()
        ag_z[2 * n].start()
        ag_z[2 * n + 1].start()
    ag_other[0, 0].start()

    load_lev.wait()
    for b in range(KV // BLOCK):
        cols = pl.ds(b * BLOCK, BLOCK)
        lev[:, cols] = (lev[:, cols].astype(f32) * scales[:, b : b + 1]).astype(bf16)
    for copy in y_part:
        copy.start()

    def normalize(first):
        def body(n, carry):
            rows = pl.ds(pl.multiple_of(first + n * 16, 16), 16)
            total = jnp.zeros((16, 128), f32)
            for k in range(D // 128):
                v = tok[rows, k * 128 : (k + 1) * 128].astype(f32)
                total += v * v
            spread = jnp.sum(total, axis=1, keepdims=True) / D
            inv = lax.rsqrt(spread + norm_eps)
            for k in range(D // 128):
                cols = pl.ds(k * 128, 128)
                v = tok[rows, cols].astype(f32)
                tok[rows, cols] = (v * inv * gain[:, cols]).astype(bf16)
            return carry

        lax.fori_loop(0, CHUNK // 16, body, 0)

    for n in range(ROWS // CHUNK):
        loads[n].wait()
        normalize(n * CHUNK)
        if n == 3:
            ag_right[0, 0].wait_recv()
            ag_relay[0, 0].start()
            ag_left[0, 1].wait_recv()
            ag_relay[0, 1].start()

    def columns(dz, dx, dc):
        return pl.ds(pl.multiple_of(fs(dz, dx, dc) * ROWS, ROWS), ROWS)

    def gradient(dz, dx, dc):
        return lax.dot_general(
            tok[:, columns(dz, dx, dc)],
            cot[...],
            (((0,), (0,)), ((), ())),
            preferred_element_type=f32,
        )

    def gradients(zz):
        def give(n, carry):
            dx = (2 + n) % 4
            p_out[zz, dx] = gradient(zz, dx, 1).astype(bf16)
            pair(zz, dx).start()
            return carry

        lax.fori_loop(0, 4, give, 0)

        def keep(n, carry):
            dx = (2 + n) % 4
            pair(zz, dx).wait_recv()
            q[zz, dx] = (gradient(zz, dx, 0) + p_in[zz, dx].astype(f32)).astype(bf16)
            return carry

        lax.fori_loop(0, 4, keep, 0)

    def scatter(zz):
        opp_left[zz].start()
        opp_right[zz].start()
        dir_right[zz].start()
        dir_left[zz].start()

    def scatter_sums(zz):
        opp_right[zz].wait_recv()
        q[zz, 1, high] = (q[zz, 1, high].astype(f32) + r_b[zz].astype(f32)).astype(bf16)
        for n in range(2):
            sum_right[zz, n].start()
        opp_left[zz].wait_recv()
        q[zz, 3, low] = (q[zz, 3, low].astype(f32) + r_a[zz].astype(f32)).astype(bf16)
        for n in range(2):
            sum_left[zz, n].start()

    def key_block(zz, dx, dc):
        return jnp.dot(tok[:, columns(zz, dx, dc)], wg[zz, dx, dc], preferred_element_type=f32)

    def key_pair(zz, dx, first=False):
        ag_other[zz, dx].wait_recv()

        def body(dc, carry):
            acc[...] += key_block(zz, dx, dc)
            return carry

        if first:
            acc[...] = jnp.zeros_like(acc)
        lax.fori_loop(0, 2, body, 0)

    def relay(zz, n):
        (ag_right if n % 2 == 0 else ag_left)[zz, n].wait_recv()
        ag_relay[zz, n].start()

    relay(0, 2)
    relay(0, 3)
    load_cot.wait()
    gradients(1)
    scatter(1)

    for copy in y_part:
        copy.wait_recv()
    part = lev[mine].astype(f32)
    for d in range(3):
        part += y_in[d].astype(f32)
    zl_in[zl] = part.astype(bf16)
    for copy in zl_part:
        copy.start()

    for n in (1, 3):
        ag_right[0, n].wait_recv()
    ag_other[0, 3].start()
    for n in (0, 2):
        ag_left[0, n].wait_recv()
    ag_other[0, 1].start()
    key_pair(0, 0, first=True)
    for n in range(4):
        ag_relay[0, n].wait_recv()
    ag_other[0, 2].start()

    for n in range(4):
        ag_z[n].wait_recv()
    gradients(0)
    scatter_sums(1)
    for n in range(2):
        for m in range(2):
            ag_right[1, 2 * n + m].start()
            ag_left[1, 2 * n + 1 - m].start()
    ag_other[1, 0].start()

    for copy in zl_part:
        copy.wait_recv()
    whole = zl_in[0].astype(f32)
    for d in range(1, NZ):
        whole += zl_in[d].astype(f32)
    sum_out[mine] = whole.astype(bf16)
    for copy in y_sum:
        copy.start()

    key_pair(0, 3)
    key_pair(0, 1)
    key_pair(0, 2)
    key_pair(1, 0)

    dir_right[1].wait_recv()
    dir_left[1].wait_recv()
    for n in range(2):
        sum_left[1, n].wait_recv()
        sum_right[1, n].wait_recv()
    z_out[...] = (q[1, 0].astype(f32) + from_m[1].astype(f32) + from_p[1].astype(f32)).astype(bf16)
    for n in range(4):
        z_send[n].start()

    for n in range(4):
        relay(1, n)
    scatter(0)
    for n in (1, 3):
        ag_right[1, n].wait_recv()
    ag_other[1, 3].start()
    for n in (0, 2):
        ag_left[1, n].wait_recv()
    ag_other[1, 1].start()
    key_pair(1, 3)
    key_pair(1, 1)
    scatter_sums(0)
    for n in range(4):
        ag_relay[1, n].wait_recv()
    ag_other[1, 2].start()
    key_pair(1, 2)
    keys_out[...] = acc[...].astype(bf16)

    for copy in y_sum:
        copy.wait_recv()
    for n in range(4):
        z_send[n].wait_recv()
    dir_right[0].wait_recv()
    dir_left[0].wait_recv()

    def finish(n):
        rows = quarter(n)
        total = q[0, 0, rows].astype(f32) + z_in[rows].astype(f32)
        total += from_m[0, rows].astype(f32) + from_p[0, rows].astype(f32)
        inner_out[rows] = wf[rows] - step_scale * total

    sum_left[0, 0].wait_recv()
    finish(0)
    sum_right[0, 0].wait_recv()
    finish(2)
    sum_left[0, 1].wait_recv()
    finish(1)
    sum_right[0, 1].wait_recv()
    finish(3)
    for copy in started:
        copy.wait_send()

    def drain(n, carry):
        pair(n // 4, n % 4).wait_send()
        return carry

    lax.fori_loop(0, 8, drain, 0)


N_ROLES = 160


def on_device(
    tokens_in,
    norm_gain,
    local_weights,
    cotangent,
    delta_levels,
    block_scales,
    outer_weights_in,
    momentum_in,
):
    features = tokens_in.shape[-1]
    groups = lax.axis_size("fsdp")
    islands = lax.axis_size("island")
    tokens = tokens_in[0].reshape(-1, features)
    tangent = cotangent[0].reshape(-1, cotangent.shape[-1])
    local_rows = tokens.shape[0]
    step_scale = inner_rate / math.sqrt(features) / math.sqrt(local_rows * groups)

    any_space = pl.BlockSpec(memory_space=pl.ANY)
    vmem = pl.BlockSpec(memory_space=pltpu.VMEM)
    keys, inner_weights, summed = pl.pallas_call(
        functools.partial(kernel, step_scale),
        out_shape=(
            jax.ShapeDtypeStruct((ROWS, KV), bf16),
            jax.ShapeDtypeStruct((ROWS, KV), f32),
            jax.ShapeDtypeStruct((ROWS, KV), bf16),
        ),
        in_specs=[any_space, vmem, any_space, any_space, any_space, vmem],
        out_specs=(vmem, vmem, vmem),
        scratch_shapes=[
            pltpu.VMEM((ROWS, D), bf16),
            pltpu.VMEM((ROWS, KV), f32),
            pltpu.VMEM((ROWS, KV), bf16),
            pltpu.VMEM((ROWS, KV), bf16),
            pltpu.VMEM((2, 4, 2, ROWS, KV), bf16),
            pltpu.VMEM((ROWS, KV), f32),
            pltpu.VMEM((2, 4, ROWS, KV), bf16),
            pltpu.VMEM((2, 4, ROWS, KV), bf16),
            pltpu.VMEM((2, 4, ROWS, KV), bf16),
            pltpu.VMEM((2, HALF, KV), bf16),
            pltpu.VMEM((2, HALF, KV), bf16),
            pltpu.VMEM((2, ROWS, KV), bf16),
            pltpu.VMEM((2, ROWS, KV), bf16),
            pltpu.VMEM((ROWS, KV), bf16),
            pltpu.VMEM((ROWS, KV), bf16),
            pltpu.VMEM((3, QUARTER, KV), bf16),
            pltpu.VMEM((NZ, QUARTER, KV), bf16),
            pltpu.SemaphoreType.DMA((3 + ROWS // CHUNK,)),
            pltpu.SemaphoreType.DMA((N_ROLES,)),
            pltpu.SemaphoreType.DMA((N_ROLES,)),
        ],
        compiler_params=pltpu.CompilerParams(
            collective_id=0, has_side_effects=True, vmem_limit_bytes=50 * 2**20
        ),
        cost_estimate=pl.CostEstimate(
            flops=4 * ROWS * D * KV, bytes_accessed=14 * 2**20, transcendentals=ROWS
        ),
    )(
        tokens,
        norm_gain.reshape(1, -1),
        local_weights[0],
        tangent,
        delta_levels[0],
        block_scales[0],
    )
    mean_delta = summed.astype(f32) / islands
    momentum_new = keep_rate * momentum_in + mean_delta
    weights_new = outer_weights_in - outer_rate * (mean_delta + keep_rate * momentum_new)
    merged = mix_share * inner_weights + (1.0 - mix_share) * weights_new
    return (keys.reshape(cotangent.shape), merged[None], weights_new, momentum_new)


def solution(mesh):
    in_specs = (
        P("island", None, "fsdp", None),
        P(),
        P("island", "fsdp", None),
        P("island", None, "fsdp", None),
        P("island", "fsdp", None),
        P("island", "fsdp", None),
        P("fsdp", None),
        P("fsdp", None),
    )
    out_specs = (
        P("island", None, "fsdp", None),
        P("island", "fsdp", None),
        P("fsdp", None),
        P("fsdp", None),
    )
    return jax.shard_map(
        on_device, mesh=mesh, in_specs=in_specs, out_specs=out_specs, check_vma=False
    )
```

```python
import functools
import math

import jax
import jax.numpy as jnp
from jax import lax
from jax.experimental import pallas as pl
from jax.experimental.pallas import tpu as pltpu
from jax.sharding import PartitionSpec as P

BLOCK = 128
NX = 4
NY = 4
NZ = 4
ROWS = 512
KV = 512
D = 8192
HALF = 256
QUARTER = 128
PART = 32
CHUNK = 64

norm_eps = 1e-05
inner_rate = 0.3
outer_rate = 0.7
keep_rate = 0.9
mix_share = 0.5

MESH = pl.DeviceIdType.MESH
f32 = jnp.float32
bf16 = jnp.bfloat16


def kernel(
    step_scale,
    islands,
    tok_hbm,
    gain_hbm,
    w_hbm,
    cot_hbm,
    lev_hbm,
    scales_hbm,
    ow_hbm,
    mom_hbm,
    keys_out,
    merged_out,
    ow_out,
    mom_out,
    tok,
    gain,
    wf,
    cot,
    lev,
    scales,
    wg,
    acc,
    p_out,
    p_in,
    q,
    r_a,
    r_b,
    from_m,
    from_p,
    z_out,
    z_in,
    y_in,
    zl_out,
    zl_in,
    total_delta,
    load_sem,
    send_sem,
    recv_sem,
):
    f = lax.axis_index("fsdp")
    i = lax.axis_index("island")
    zh, x, c = f // 8, (f // 2) % NX, f % 2
    zl, y = i // NY, i % NY

    def fs(dz, dx, dc):
        return ((zh + dz) % 2) * 8 + ((x + dx) % NX) * 2 + (c + dc) % 2

    def to_fsdp(dz, dx, dc):
        return {"fsdp": fs(dz, dx, dc), "island": i}

    def to_island(dzl, dy):
        return {"fsdp": f, "island": ((zl + dzl) % NZ) * NY + (y + dy) % NY}

    right, left = to_fsdp(0, 1, 0), to_fsdp(0, NX - 1, 0)
    across, other = to_fsdp(1, 0, 0), to_fsdp(0, 0, 1)

    started = []
    counter = [0]

    def remote(k, src, dst, device):
        return pltpu.make_async_remote_copy(
            src_ref=src,
            dst_ref=dst,
            send_sem=send_sem.at[k],
            recv_sem=recv_sem.at[k],
            device_id=device,
            device_id_type=MESH,
        )

    def role(src, dst, device):
        copy = remote(counter[0], src, dst, device)
        counter[0] += 1
        started.append(copy)
        return copy

    load_count = [0]

    def load(src, dst):
        copy = pltpu.make_async_copy(src, dst, load_sem.at[load_count[0]])
        load_count[0] += 1
        copy.start()
        return copy

    load_w = load(w_hbm, wf)
    load_lev = load(lev_hbm, lev)
    load_scales = load(scales_hbm, scales)
    load_gain = load(gain_hbm, gain)
    loads = []
    for n in range(ROWS // CHUNK):
        rows = pl.ds(n * CHUNK, CHUNK)
        loads.append(load(tok_hbm.at[rows], tok.at[rows]))
    load_cot = load(cot_hbm, cot)
    load_ow = load(ow_hbm, ow_out)
    load_mom = load(mom_hbm, mom_out)

    barrier = pltpu.get_barrier_semaphore()
    peers = [right, left, across, other]
    peers += [to_island(0, d) for d in (1, 2, 3)] + [to_island(d, 0) for d in (1, 2, 3)]
    for peer in peers:
        pl.semaphore_signal(barrier, inc=1, device_id=peer, device_id_type=MESH)
    load_w.wait()
    wg[0, 0, 0] = wf[...].astype(bf16)
    pl.semaphore_wait(barrier, len(peers))

    def quarter(n):
        return pl.ds(n * QUARTER, QUARTER)

    ag_right, ag_left, ag_relay, ag_other = {}, {}, {}, {}
    for zz in range(2):
        for n in (0, 1, 2, 3):
            rows = quarter(n)
            ag_right[zz, n] = role(wg.at[zz, 0, 0, rows], wg.at[zz, 3, 0, rows], right)
        for n in (1, 0, 3, 2):
            rows = quarter(n)
            ag_left[zz, n] = role(wg.at[zz, 0, 0, rows], wg.at[zz, 1, 0, rows], left)
        for n in (0, 2):
            rows = quarter(n)
            ag_relay[zz, n] = role(wg.at[zz, 3, 0, rows], wg.at[zz, 2, 0, rows], right)
        for n in (1, 3):
            rows = quarter(n)
            ag_relay[zz, n] = role(wg.at[zz, 1, 0, rows], wg.at[zz, 2, 0, rows], left)
        for dx in range(4):
            ag_other[zz, dx] = role(wg.at[zz, dx, 0], wg.at[zz, dx, 1], other)
    ag_z = [role(wg.at[0, 0, 0, quarter(n)], wg.at[1, 0, 0, quarter(n)], across) for n in range(4)]

    low, high = pl.ds(0, HALF), pl.ds(HALF, HALF)
    opp_left, opp_right, dir_right, dir_left, sum_right, sum_left = {}, {}, {}, {}, {}, {}
    for zz in range(2):
        for n in range(2):
            part, upper, lower = quarter(n), quarter(n), quarter(2 + n)
            opp_left[zz, n] = role(q.at[zz, 2, upper], r_a.at[zz, part], left)
            opp_right[zz, n] = role(q.at[zz, 2, lower], r_b.at[zz, part], right)
            sum_left[zz, n] = role(q.at[zz, 3, upper], from_p.at[zz, upper], left)
            sum_right[zz, n] = role(q.at[zz, 1, lower], from_m.at[zz, lower], right)
        dir_right[zz] = role(q.at[zz, 1, low], from_m.at[zz, low], right)
        dir_left[zz] = role(q.at[zz, 3, high], from_p.at[zz, high], left)
    z_send = [role(z_out.at[quarter(n)], z_in.at[quarter(n)], across) for n in range(4)]

    def y_rows(d):
        return pl.ds(pl.multiple_of(((y + d) % NY) * QUARTER, QUARTER), QUARTER)

    def z_rows(d):
        return pl.ds(pl.multiple_of(((zl + d) % NZ) * PART, PART), PART)

    mine = y_rows(0)
    my_part = pl.ds(pl.multiple_of(y * QUARTER + zl * PART, PART), PART)
    steps = (1, 2, 3)
    y_part = [role(lev.at[y_rows(d)], y_in.at[d - 1], to_island(0, d)) for d in steps]
    zl_part = [role(zl_out.at[z_rows(d)], zl_in.at[d - 1], to_island(d, 0)) for d in steps]
    zl_sum = [role(total_delta.at[my_part], total_delta.at[my_part], to_island(d, 0)) for d in steps]
    y_sum = [role(total_delta.at[mine], total_delta.at[mine], to_island(0, d)) for d in steps]

    base = counter[0]

    def pair(zz, dx):
        return remote(base + zz * 4 + dx, p_out.at[zz, dx], p_in.at[zz, dx], other)

    for n in range(2):
        for m in range(2):
            ag_right[0, 2 * n + m].start()
            ag_left[0, 2 * n + 1 - m].start()
    for n in range(4):
        ag_z[n].start()
    ag_other[0, 0].start()

    load_lev.wait()
    load_scales.wait()
    by_block = scales[...]
    by_row = jnp.transpose(jnp.concatenate([by_block, by_block], axis=0))
    for b in range(KV // BLOCK):
        cols = pl.ds(b * BLOCK, BLOCK)
        lev[:, cols] = (lev[:, cols].astype(f32) * by_row[:, b : b + 1]).astype(bf16)
    for copy in y_part:
        copy.start()

    def normalize(first):
        def body(n, carry):
            rows = pl.ds(pl.multiple_of(first + n * 16, 16), 16)
            total = jnp.zeros((16, 128), f32)
            for k in range(D // 128):
                v = tok[rows, k * 128 : (k + 1) * 128].astype(f32)
                total += v * v
            spread = jnp.sum(total, axis=1, keepdims=True) / D
            inv = lax.rsqrt(spread + norm_eps)
            for k in range(D // 128):
                cols = pl.ds(k * 128, 128)
                v = tok[rows, cols].astype(f32)
                tok[rows, cols] = (v * inv * gain[:, cols]).astype(bf16)
            return carry

        lax.fori_loop(0, CHUNK // 16, body, 0)

    def relay(zz, n):
        (ag_right if n % 2 == 0 else ag_left)[zz, n].wait_recv()
        ag_relay[zz, n].start()

    load_gain.wait()
    for n in range(ROWS // CHUNK):
        loads[n].wait()
        normalize(n * CHUNK)
        if n == 3:
            relay(0, 0)
            relay(0, 1)
    relay(0, 2)
    relay(0, 3)

    def columns(dz, dx, dc):
        return pl.ds(pl.multiple_of(fs(dz, dx, dc) * ROWS, ROWS), ROWS)

    def gradient(dz, dx, dc):
        return lax.dot_general(
            tok[:, columns(dz, dx, dc)],
            cot[...],
            (((0,), (0,)), ((), ())),
            preferred_element_type=f32,
        )

    def give_gradients(zz):
        def give(n, carry):
            dx = (2 + n) % 4
            p_out[zz, dx] = gradient(zz, dx, 1).astype(bf16)
            pair(zz, dx).start()
            return carry

        lax.fori_loop(0, 4, give, 0)

    def keep_gradients(zz, first, last):
        def keep(n, carry):
            dx = (2 + n) % 4
            pair(zz, dx).wait_recv()
            q[zz, dx] = (gradient(zz, dx, 0) + p_in[zz, dx].astype(f32)).astype(bf16)
            return carry

        lax.fori_loop(first, last, keep, 0)

    def scatter_opposite(zz):
        for n in range(2):
            opp_right[zz, n].start()
            opp_left[zz, n].start()

    def scatter_direct(zz):
        dir_right[zz].start()
        dir_left[zz].start()

    def scatter_sums(zz):
        for n in range(2):
            part, upper, lower = quarter(n), quarter(n), quarter(2 + n)
            opp_right[zz, n].wait_recv()
            q[zz, 1, lower] = (q[zz, 1, lower].astype(f32) + r_b[zz, part].astype(f32)).astype(bf16)
            sum_right[zz, n].start()
            opp_left[zz, n].wait_recv()
            q[zz, 3, upper] = (q[zz, 3, upper].astype(f32) + r_a[zz, part].astype(f32)).astype(bf16)
            sum_left[zz, n].start()

    def key_pair(zz, dx, first=False):
        ag_other[zz, dx].wait_recv()

        def body(dc, carry):
            acc[...] += jnp.dot(
                tok[:, columns(zz, dx, dc)], wg[zz, dx, dc], preferred_element_type=f32
            )
            return carry

        if first:
            acc[...] = jnp.zeros_like(acc)
        lax.fori_loop(0, 2, body, 0)

    def share_neighbours(zz):
        for n in (1, 3):
            ag_right[zz, n].wait_recv()
        ag_other[zz, 3].start()
        for n in (0, 2):
            ag_left[zz, n].wait_recv()
        ag_other[zz, 1].start()

    def share_opposite(zz):
        for n in range(4):
            ag_relay[zz, n].wait_recv()
        ag_other[zz, 2].start()

    for copy in y_part:
        copy.wait_recv()
    part = lev[mine].astype(f32)
    for d in range(3):
        part += y_in[d].astype(f32)
    zl_out[...] = part.astype(bf16)
    for copy in zl_part:
        copy.start()

    load_cot.wait()
    give_gradients(1)
    keep_gradients(1, 0, 1)
    scatter_opposite(1)
    keep_gradients(1, 1, 4)
    scatter_direct(1)
    share_neighbours(0)

    for copy in zl_part:
        copy.wait_recv()
    part = zl_out[z_rows(0)].astype(f32)
    for d in range(3):
        part += zl_in[d].astype(f32)
    total_delta[my_part] = part.astype(bf16)
    for copy in zl_sum:
        copy.start()

    key_pair(0, 0, first=True)
    give_gradients(0)
    scatter_sums(1)
    share_opposite(0)
    keep_gradients(0, 0, 4)
    for copy in zl_sum:
        copy.wait_recv()
    for copy in y_sum:
        copy.start()
    key_pair(0, 3)
    key_pair(0, 1)

    dir_right[1].wait_recv()
    dir_left[1].wait_recv()
    for n in range(4):
        ag_z[n].wait_recv()

    def send_across(n):
        rows = quarter(n)
        total = q[1, 0, rows].astype(f32) + from_m[1, rows].astype(f32)
        z_out[rows] = (total + from_p[1, rows].astype(f32)).astype(bf16)
        z_send[n].start()

    for n in range(2):
        sum_left[1, n].wait_recv()
        send_across(n)
        sum_right[1, n].wait_recv()
        send_across(2 + n)
        if n == 0:
            for m in range(2):
                for k in range(2):
                    ag_right[1, 2 * m + k].start()
                    ag_left[1, 2 * m + 1 - k].start()
            ag_other[1, 0].start()

    key_pair(0, 2)
    relay(1, 0)
    relay(1, 1)

    load_ow.wait()
    load_mom.wait()
    for copy in y_sum:
        copy.wait_recv()

    def outer(n, carry):
        rows = pl.ds(pl.multiple_of(n * PART, PART), PART)
        mean = total_delta[rows].astype(f32) / islands
        momentum = keep_rate * mom_out[rows] + mean
        mom_out[rows] = momentum
        ow_out[rows] = ow_out[rows] - outer_rate * (mean + keep_rate * momentum)
        return carry

    lax.fori_loop(0, ROWS // PART, outer, 0)

    key_pair(1, 0)
    relay(1, 2)
    relay(1, 3)
    scatter_opposite(0)
    scatter_direct(0)
    share_neighbours(1)
    key_pair(1, 3)
    key_pair(1, 1)
    scatter_sums(0)
    share_opposite(1)
    key_pair(1, 2)
    keys_out[...] = acc[...].astype(bf16)

    for n in range(4):
        z_send[n].wait_recv()
    dir_right[0].wait_recv()
    dir_left[0].wait_recv()

    def finish(n):
        rows = quarter(n)
        total = q[0, 0, rows].astype(f32) + z_in[rows].astype(f32)
        total += from_m[0, rows].astype(f32) + from_p[0, rows].astype(f32)
        inner = wf[rows] - step_scale * total
        merged_out[rows] = mix_share * inner + (1.0 - mix_share) * ow_out[rows]

    for n in range(2):
        sum_left[0, n].wait_recv()
        finish(n)
        sum_right[0, n].wait_recv()
        finish(2 + n)
    for copy in started:
        copy.wait_send()

    def drain(n, carry):
        pair(n // 4, n % 4).wait_send()
        return carry

    lax.fori_loop(0, 8, drain, 0)


def write(keys, merged, weights, momentum, keys_hbm, merged_hbm, weights_hbm, momentum_hbm, sem):
    pairs = ((merged, merged_hbm), (weights, weights_hbm), (momentum, momentum_hbm), (keys, keys_hbm))
    copies = [pltpu.make_async_copy(a, b, sem.at[n]) for n, (a, b) in enumerate(pairs)]
    for copy in copies:
        copy.start()
    for copy in copies:
        copy.wait()


N_ROLES = 160


def on_device(
    tokens_in,
    norm_gain,
    local_weights,
    cotangent,
    delta_levels,
    block_scales,
    outer_weights_in,
    momentum_in,
):
    features = tokens_in.shape[-1]
    groups = lax.axis_size("fsdp")
    islands = lax.axis_size("island")
    tokens = tokens_in[0].reshape(-1, features)
    tangent = cotangent[0].reshape(-1, cotangent.shape[-1])
    local_rows = tokens.shape[0]
    step_scale = inner_rate / math.sqrt(features) / math.sqrt(local_rows * groups)

    hbm = pl.BlockSpec(memory_space=pltpu.HBM)
    vmem = pl.BlockSpec(memory_space=pltpu.VMEM)
    shapes = (
        jax.ShapeDtypeStruct((ROWS, KV), bf16),
        jax.ShapeDtypeStruct((ROWS, KV), f32),
        jax.ShapeDtypeStruct((ROWS, KV), f32),
        jax.ShapeDtypeStruct((ROWS, KV), f32),
    )
    results = pl.pallas_call(
        functools.partial(kernel, step_scale, islands),
        out_shape=tuple(pltpu.VMEM(s.shape, s.dtype) for s in shapes),
        in_specs=[hbm] * 8,
        out_specs=(vmem,) * 4,
        scratch_shapes=[
            pltpu.VMEM((ROWS, D), bf16),
            pltpu.VMEM((1, D), f32),
            pltpu.VMEM((ROWS, KV), f32),
            pltpu.VMEM((ROWS, KV), bf16),
            pltpu.VMEM((ROWS, KV), bf16),
            pltpu.VMEM((KV // BLOCK, ROWS), f32),
            pltpu.VMEM((2, 4, 2, ROWS, KV), bf16),
            pltpu.VMEM((ROWS, KV), f32),
            pltpu.VMEM((2, 4, ROWS, KV), bf16),
            pltpu.VMEM((2, 4, ROWS, KV), bf16),
            pltpu.VMEM((2, 4, ROWS, KV), bf16),
            pltpu.VMEM((2, HALF, KV), bf16),
            pltpu.VMEM((2, HALF, KV), bf16),
            pltpu.VMEM((2, ROWS, KV), bf16),
            pltpu.VMEM((2, ROWS, KV), bf16),
            pltpu.VMEM((ROWS, KV), bf16),
            pltpu.VMEM((ROWS, KV), bf16),
            pltpu.VMEM((3, QUARTER, KV), bf16),
            pltpu.VMEM((QUARTER, KV), bf16),
            pltpu.VMEM((3, PART, KV), bf16),
            pltpu.VMEM((ROWS, KV), bf16),
            pltpu.SemaphoreType.DMA((7 + ROWS // CHUNK,)),
            pltpu.SemaphoreType.DMA((N_ROLES,)),
            pltpu.SemaphoreType.DMA((N_ROLES,)),
        ],
        compiler_params=pltpu.CompilerParams(
            collective_id=0, has_side_effects=True, vmem_limit_bytes=56 * 2**20
        ),
        cost_estimate=pl.CostEstimate(
            flops=4 * ROWS * D * KV, bytes_accessed=14 * 2**20, transcendentals=ROWS
        ),
    )(
        tokens,
        norm_gain.reshape(1, -1),
        local_weights[0],
        tangent,
        delta_levels[0],
        block_scales[0].T,
        outer_weights_in,
        momentum_in,
    )
    keys, merged, weights_new, momentum_new = pl.pallas_call(
        write,
        out_shape=shapes,
        in_specs=[vmem] * 4,
        out_specs=(hbm,) * 4,
        scratch_shapes=[pltpu.SemaphoreType.DMA((4,))],
        compiler_params=pltpu.CompilerParams(vmem_limit_bytes=2**20),
    )(*results)
    return (keys.reshape(cotangent.shape), merged[None], weights_new, momentum_new)


def solution(mesh):
    in_specs = (
        P("island", None, "fsdp", None),
        P(),
        P("island", "fsdp", None),
        P("island", None, "fsdp", None),
        P("island", "fsdp", None),
        P("island", "fsdp", None),
        P("fsdp", None),
        P("fsdp", None),
    )
    out_specs = (
        P("island", None, "fsdp", None),
        P("island", "fsdp", None),
        P("fsdp", None),
        P("fsdp", None),
    )
    return jax.shard_map(
        on_device, mesh=mesh, in_specs=in_specs, out_specs=out_specs, check_vma=False
    )
```

```python
import functools
import math

import jax
import jax.numpy as jnp
from jax import lax
from jax.experimental import pallas as pl
from jax.experimental.pallas import tpu as pltpu
from jax.sharding import PartitionSpec as P

BLOCK = 128
NX = 4
NY = 4
NZ = 4
ROWS = 512
KV = 512
D = 8192
HALF = 256
QUARTER = 128
PART = 32
MEET_AFTER = 1
RELAY_AFTER = 4
CHUNK = 64

norm_eps = 1e-05
inner_rate = 0.3
outer_rate = 0.7
keep_rate = 0.9
mix_share = 0.5

MESH = pl.DeviceIdType.MESH
f32 = jnp.float32
bf16 = jnp.bfloat16


def kernel(
    step_scale,
    islands,
    tok_hbm,
    gain_hbm,
    w_hbm,
    cot_hbm,
    lev_hbm,
    scales_hbm,
    ow_hbm,
    mom_hbm,
    keys_out,
    merged_out,
    ow_out,
    mom_out,
    tok,
    gain,
    wf,
    cot,
    lev,
    scales,
    wg,
    acc,
    p_out,
    p_in,
    q,
    r_a,
    r_b,
    from_m,
    from_p,
    z_out,
    z_in,
    y_in,
    zl_out,
    zl_in,
    total_delta,
    load_sem,
    send_sem,
    recv_sem,
    near_sem,
    far_sem,
):
    f = lax.axis_index("fsdp")
    i = lax.axis_index("island")
    zh, x, c = f // 8, (f // 2) % NX, f % 2
    zl, y = i // NY, i % NY

    def fs(dz, dx, dc):
        return ((zh + dz) % 2) * 8 + ((x + dx) % NX) * 2 + (c + dc) % 2

    def to_fsdp(dz, dx, dc):
        return {"fsdp": fs(dz, dx, dc), "island": i}

    def to_island(dzl, dy):
        return {"fsdp": f, "island": ((zl + dzl) % NZ) * NY + (y + dy) % NY}

    right, left = to_fsdp(0, 1, 0), to_fsdp(0, NX - 1, 0)
    across, other = to_fsdp(1, 0, 0), to_fsdp(0, 0, 1)

    started = []
    counter = [0]

    def remote(k, src, dst, device):
        return pltpu.make_async_remote_copy(
            src_ref=src,
            dst_ref=dst,
            send_sem=send_sem.at[k],
            recv_sem=recv_sem.at[k],
            device_id=device,
            device_id_type=MESH,
        )

    def role(src, dst, device):
        copy = remote(counter[0], src, dst, device)
        counter[0] += 1
        started.append(copy)
        return copy

    load_count = [0]

    def load(src, dst):
        copy = pltpu.make_async_copy(src, dst, load_sem.at[load_count[0]])
        load_count[0] += 1
        copy.start()
        return copy

    load_w = load(w_hbm, wf)
    load_lev = load(lev_hbm, lev)
    load_scales = load(scales_hbm, scales)
    load_gain = load(gain_hbm, gain)
    loads = []
    for n in range(ROWS // CHUNK):
        rows = pl.ds(n * CHUNK, CHUNK)
        loads.append(load(tok_hbm.at[rows], tok.at[rows]))
    load_cot = load(cot_hbm, cot)
    load_ow = load(ow_hbm, ow_out)
    load_mom = load(mom_hbm, mom_out)

    barrier = pltpu.get_barrier_semaphore()

    def at_core(device, core):
        return {"fsdp": (device["fsdp"] // 2) * 2 + core, "island": device["island"]}

    near = [right, left]
    far = [across]
    far += [to_island(0, d) for d in (1, 2, 3)] + [to_island(d, 0) for d in (1, 2, 3)]
    pl.semaphore_signal(barrier, inc=1, device_id=other, device_id_type=MESH)
    for core, group in ((0, near), (1, far)):
        for peer in group:
            pl.semaphore_signal(
                barrier, inc=1, device_id=at_core(peer, core), device_id_type=MESH
            )
    load_w.wait()
    wg[0, 0, 0] = wf[...].astype(bf16)

    @pl.when(c == 0)
    def _():
        pl.semaphore_wait(barrier, 1 + 2 * len(near))
        pl.semaphore_signal(near_sem, inc=1, device_id=other, device_id_type=MESH)

    @pl.when(c == 1)
    def _():
        pl.semaphore_wait(near_sem, 1)

    def quarter(n):
        return pl.ds(n * QUARTER, QUARTER)

    ag_right, ag_left, ag_relay, ag_other = {}, {}, {}, {}
    for zz in range(2):
        for n in (0, 1, 2, 3):
            rows = quarter(n)
            ag_right[zz, n] = role(wg.at[zz, 0, 0, rows], wg.at[zz, 3, 0, rows], right)
        for n in (1, 0, 3, 2):
            rows = quarter(n)
            ag_left[zz, n] = role(wg.at[zz, 0, 0, rows], wg.at[zz, 1, 0, rows], left)
        for n in (0, 2):
            rows = quarter(n)
            ag_relay[zz, n] = role(wg.at[zz, 3, 0, rows], wg.at[zz, 2, 0, rows], right)
        for n in (1, 3):
            rows = quarter(n)
            ag_relay[zz, n] = role(wg.at[zz, 1, 0, rows], wg.at[zz, 2, 0, rows], left)
        for dx in range(4):
            ag_other[zz, dx] = role(wg.at[zz, dx, 0], wg.at[zz, dx, 1], other)
    ag_z = [role(wg.at[0, 0, 0, quarter(n)], wg.at[1, 0, 0, quarter(n)], across) for n in range(4)]

    low, high = pl.ds(0, HALF), pl.ds(HALF, HALF)
    opp_left, opp_right, dir_right, dir_left, sum_right, sum_left = {}, {}, {}, {}, {}, {}
    for zz in range(2):
        for n in range(2):
            part, upper, lower = quarter(n), quarter(n), quarter(2 + n)
            opp_left[zz, n] = role(q.at[zz, 2, upper], r_a.at[zz, part], left)
            opp_right[zz, n] = role(q.at[zz, 2, lower], r_b.at[zz, part], right)
            sum_left[zz, n] = role(q.at[zz, 3, upper], from_p.at[zz, upper], left)
            sum_right[zz, n] = role(q.at[zz, 1, lower], from_m.at[zz, lower], right)
        dir_right[zz] = role(q.at[zz, 1, low], from_m.at[zz, low], right)
        dir_left[zz] = role(q.at[zz, 3, high], from_p.at[zz, high], left)
    z_send = [role(z_out.at[quarter(n)], z_in.at[quarter(n)], across) for n in range(4)]

    def y_rows(d):
        return pl.ds(pl.multiple_of(((y + d) % NY) * QUARTER, QUARTER), QUARTER)

    def z_rows(d):
        return pl.ds(pl.multiple_of(((zl + d) % NZ) * PART, PART), PART)

    mine = y_rows(0)
    my_part = pl.ds(pl.multiple_of(y * QUARTER + zl * PART, PART), PART)
    steps = (1, 2, 3)
    y_part = [role(lev.at[y_rows(d)], y_in.at[d - 1], to_island(0, d)) for d in steps]
    zl_part = [role(zl_out.at[z_rows(d)], zl_in.at[d - 1], to_island(d, 0)) for d in steps]
    zl_sum = [role(total_delta.at[my_part], total_delta.at[my_part], to_island(d, 0)) for d in steps]
    y_sum = [role(total_delta.at[mine], total_delta.at[mine], to_island(0, d)) for d in steps]

    base = counter[0]

    def pair(zz, dx):
        return remote(base + zz * 4 + dx, p_out.at[zz, dx], p_in.at[zz, dx], other)

    def gather_right_left(zz, n):
        for m in range(2):
            ag_right[zz, 2 * n + m].start()
            ag_left[zz, 2 * n + 1 - m].start()

    gather_right_left(0, 0)
    ag_other[0, 0].start()

    load_lev.wait()
    load_scales.wait()
    by_block = scales[...]
    by_row = jnp.transpose(jnp.concatenate([by_block, by_block], axis=0))
    for b in range(KV // BLOCK):
        cols = pl.ds(b * BLOCK, BLOCK)
        lev[:, cols] = (lev[:, cols].astype(f32) * by_row[:, b : b + 1]).astype(bf16)

    def normalize(first):
        def body(n, carry):
            rows = pl.ds(pl.multiple_of(first + n * 16, 16), 16)
            total = jnp.zeros((16, 128), f32)
            for k in range(D // 128):
                v = tok[rows, k * 128 : (k + 1) * 128].astype(f32)
                total += v * v
            spread = jnp.sum(total, axis=1, keepdims=True) / D
            inv = lax.rsqrt(spread + norm_eps)
            for k in range(D // 128):
                cols = pl.ds(k * 128, 128)
                v = tok[rows, cols].astype(f32)
                tok[rows, cols] = (v * inv * gain[:, cols]).astype(bf16)
            return carry

        lax.fori_loop(0, CHUNK // 16, body, 0)

    def relay(zz, n):
        (ag_right if n % 2 == 0 else ag_left)[zz, n].wait_recv()
        ag_relay[zz, n].start()

    def meet_far():
        @pl.when(c == 1)
        def _():
            pl.semaphore_wait(barrier, 1 + 2 * len(far))
            pl.semaphore_signal(far_sem, inc=1, device_id=other, device_id_type=MESH)

        @pl.when(c == 0)
        def _():
            pl.semaphore_wait(far_sem, 1)

        for n in range(2):
            ag_z[n].start()
        gather_right_left(0, 1)
        for copy in y_part:
            copy.start()

    load_gain.wait()
    for n in range(ROWS // CHUNK):
        loads[n].wait()
        normalize(n * CHUNK)
        if n == MEET_AFTER:
            meet_far()
        if n == RELAY_AFTER:
            relay(0, 0)
            relay(0, 1)
    relay(0, 2)
    relay(0, 3)

    def columns(dz, dx, dc):
        return pl.ds(pl.multiple_of(fs(dz, dx, dc) * ROWS, ROWS), ROWS)

    def gradient(dz, dx, dc):
        return lax.dot_general(
            tok[:, columns(dz, dx, dc)],
            cot[...],
            (((0,), (0,)), ((), ())),
            preferred_element_type=f32,
        )

    def give_gradients(zz):
        def give(n, carry):
            dx = (2 + n) % 4
            p_out[zz, dx] = gradient(zz, dx, 1).astype(bf16)
            pair(zz, dx).start()
            return carry

        lax.fori_loop(0, 4, give, 0)

    def keep_gradients(zz, first, last):
        def keep(n, carry):
            dx = (2 + n) % 4
            pair(zz, dx).wait_recv()
            q[zz, dx] = (gradient(zz, dx, 0) + p_in[zz, dx].astype(f32)).astype(bf16)
            return carry

        lax.fori_loop(first, last, keep, 0)

    def scatter_opposite(zz):
        for n in range(2):
            opp_right[zz, n].start()
            opp_left[zz, n].start()

    def scatter_direct(zz):
        dir_right[zz].start()
        dir_left[zz].start()

    def scatter_sums(zz):
        for n in range(2):
            part, upper, lower = quarter(n), quarter(n), quarter(2 + n)
            opp_right[zz, n].wait_recv()
            q[zz, 1, lower] = (q[zz, 1, lower].astype(f32) + r_b[zz, part].astype(f32)).astype(bf16)
            sum_right[zz, n].start()
            opp_left[zz, n].wait_recv()
            q[zz, 3, upper] = (q[zz, 3, upper].astype(f32) + r_a[zz, part].astype(f32)).astype(bf16)
            sum_left[zz, n].start()

    def key_pair(zz, dx, first=False):
        ag_other[zz, dx].wait_recv()

        def body(dc, carry):
            acc[...] += jnp.dot(
                tok[:, columns(zz, dx, dc)], wg[zz, dx, dc], preferred_element_type=f32
            )
            return carry

        if first:
            acc[...] = jnp.zeros_like(acc)
        lax.fori_loop(0, 2, body, 0)

    def share_neighbours(zz):
        for n in (1, 3):
            ag_right[zz, n].wait_recv()
        ag_other[zz, 3].start()
        for n in (0, 2):
            ag_left[zz, n].wait_recv()
        ag_other[zz, 1].start()

    def share_opposite(zz):
        for n in range(4):
            ag_relay[zz, n].wait_recv()
        ag_other[zz, 2].start()

    load_cot.wait()
    give_gradients(1)

    for copy in y_part:
        copy.wait_recv()
    part = lev[mine].astype(f32)
    for d in range(3):
        part += y_in[d].astype(f32)
    zl_out[...] = part.astype(bf16)
    for copy in zl_part:
        copy.start()

    for n in (2, 3):
        ag_z[n].start()

    keep_gradients(1, 0, 1)
    scatter_opposite(1)
    keep_gradients(1, 1, 4)
    scatter_direct(1)
    share_neighbours(0)

    key_pair(0, 0, first=True)
    give_gradients(0)
    scatter_sums(1)
    share_opposite(0)
    keep_gradients(0, 0, 4)

    for copy in zl_part:
        copy.wait_recv()
    part = zl_out[z_rows(0)].astype(f32)
    for d in range(3):
        part += zl_in[d].astype(f32)
    total_delta[my_part] = part.astype(bf16)
    for copy in zl_sum:
        copy.start()

    key_pair(0, 3)
    key_pair(0, 1)

    for copy in zl_sum:
        copy.wait_recv()
    for copy in y_sum:
        copy.start()

    dir_right[1].wait_recv()
    dir_left[1].wait_recv()
    for n in range(4):
        ag_z[n].wait_recv()

    def send_across(n):
        rows = quarter(n)
        total = q[1, 0, rows].astype(f32) + from_m[1, rows].astype(f32)
        z_out[rows] = (total + from_p[1, rows].astype(f32)).astype(bf16)
        z_send[n].start()

    for n in range(2):
        sum_left[1, n].wait_recv()
        send_across(n)
        sum_right[1, n].wait_recv()
        send_across(2 + n)
        if n == 0:
            for m in range(2):
                gather_right_left(1, m)
            ag_other[1, 0].start()

    key_pair(0, 2)
    relay(1, 0)
    relay(1, 1)

    key_pair(1, 0)
    relay(1, 2)
    relay(1, 3)
    scatter_opposite(0)
    scatter_direct(0)
    share_neighbours(1)
    key_pair(1, 3)
    key_pair(1, 1)
    scatter_sums(0)

    load_ow.wait()
    load_mom.wait()
    for copy in y_sum:
        copy.wait_recv()

    def outer(n, carry):
        rows = pl.ds(pl.multiple_of(n * PART, PART), PART)
        mean = total_delta[rows].astype(f32) / islands
        momentum = keep_rate * mom_out[rows] + mean
        mom_out[rows] = momentum
        ow_out[rows] = ow_out[rows] - outer_rate * (mean + keep_rate * momentum)
        return carry

    lax.fori_loop(0, ROWS // PART, outer, 0)

    share_opposite(1)
    key_pair(1, 2)
    keys_out[...] = acc[...].astype(bf16)

    for n in range(4):
        z_send[n].wait_recv()
    dir_right[0].wait_recv()
    dir_left[0].wait_recv()

    def finish(n):
        rows = quarter(n)
        total = q[0, 0, rows].astype(f32) + z_in[rows].astype(f32)
        total += from_m[0, rows].astype(f32) + from_p[0, rows].astype(f32)
        inner = wf[rows] - step_scale * total
        merged_out[rows] = mix_share * inner + (1.0 - mix_share) * ow_out[rows]

    for n in range(2):
        sum_left[0, n].wait_recv()
        finish(n)
        sum_right[0, n].wait_recv()
        finish(2 + n)
    for copy in started:
        copy.wait_send()

    def drain(n, carry):
        pair(n // 4, n % 4).wait_send()
        return carry

    lax.fori_loop(0, 8, drain, 0)


def write(keys, merged, weights, momentum, keys_hbm, merged_hbm, weights_hbm, momentum_hbm, sem):
    pairs = ((merged, merged_hbm), (weights, weights_hbm), (momentum, momentum_hbm), (keys, keys_hbm))
    copies = [pltpu.make_async_copy(a, b, sem.at[n]) for n, (a, b) in enumerate(pairs)]
    for copy in copies:
        copy.start()
    for copy in copies:
        copy.wait()


N_ROLES = 160


def on_device(
    tokens_in,
    norm_gain,
    local_weights,
    cotangent,
    delta_levels,
    block_scales,
    outer_weights_in,
    momentum_in,
):
    features = tokens_in.shape[-1]
    groups = lax.axis_size("fsdp")
    islands = lax.axis_size("island")
    tokens = tokens_in[0].reshape(-1, features)
    tangent = cotangent[0].reshape(-1, cotangent.shape[-1])
    local_rows = tokens.shape[0]
    step_scale = inner_rate / math.sqrt(features) / math.sqrt(local_rows * groups)

    hbm = pl.BlockSpec(memory_space=pltpu.HBM)
    vmem = pl.BlockSpec(memory_space=pltpu.VMEM)
    shapes = (
        jax.ShapeDtypeStruct((ROWS, KV), bf16),
        jax.ShapeDtypeStruct((ROWS, KV), f32),
        jax.ShapeDtypeStruct((ROWS, KV), f32),
        jax.ShapeDtypeStruct((ROWS, KV), f32),
    )
    results = pl.pallas_call(
        functools.partial(kernel, step_scale, islands),
        out_shape=tuple(pltpu.VMEM(s.shape, s.dtype) for s in shapes),
        in_specs=[hbm] * 8,
        out_specs=(vmem,) * 4,
        scratch_shapes=[
            pltpu.VMEM((ROWS, D), bf16),
            pltpu.VMEM((1, D), f32),
            pltpu.VMEM((ROWS, KV), f32),
            pltpu.VMEM((ROWS, KV), bf16),
            pltpu.VMEM((ROWS, KV), bf16),
            pltpu.VMEM((KV // BLOCK, ROWS), f32),
            pltpu.VMEM((2, 4, 2, ROWS, KV), bf16),
            pltpu.VMEM((ROWS, KV), f32),
            pltpu.VMEM((2, 4, ROWS, KV), bf16),
            pltpu.VMEM((2, 4, ROWS, KV), bf16),
            pltpu.VMEM((2, 4, ROWS, KV), bf16),
            pltpu.VMEM((2, HALF, KV), bf16),
            pltpu.VMEM((2, HALF, KV), bf16),
            pltpu.VMEM((2, ROWS, KV), bf16),
            pltpu.VMEM((2, ROWS, KV), bf16),
            pltpu.VMEM((ROWS, KV), bf16),
            pltpu.VMEM((ROWS, KV), bf16),
            pltpu.VMEM((3, QUARTER, KV), bf16),
            pltpu.VMEM((QUARTER, KV), bf16),
            pltpu.VMEM((3, PART, KV), bf16),
            pltpu.VMEM((ROWS, KV), bf16),
            pltpu.SemaphoreType.DMA((7 + ROWS // CHUNK,)),
            pltpu.SemaphoreType.DMA((N_ROLES,)),
            pltpu.SemaphoreType.DMA((N_ROLES,)),
            pltpu.SemaphoreType.REGULAR,
            pltpu.SemaphoreType.REGULAR,
        ],
        compiler_params=pltpu.CompilerParams(
            collective_id=0, has_side_effects=True, vmem_limit_bytes=56 * 2**20
        ),
        cost_estimate=pl.CostEstimate(
            flops=4 * ROWS * D * KV, bytes_accessed=14 * 2**20, transcendentals=ROWS
        ),
    )(
        tokens,
        norm_gain.reshape(1, -1),
        local_weights[0],
        tangent,
        delta_levels[0],
        block_scales[0].T,
        outer_weights_in,
        momentum_in,
    )
    keys, merged, weights_new, momentum_new = pl.pallas_call(
        write,
        out_shape=shapes,
        in_specs=[vmem] * 4,
        out_specs=(hbm,) * 4,
        scratch_shapes=[pltpu.SemaphoreType.DMA((4,))],
        compiler_params=pltpu.CompilerParams(vmem_limit_bytes=2**20),
    )(*results)
    return (keys.reshape(cotangent.shape), merged[None], weights_new, momentum_new)


def solution(mesh):
    in_specs = (
        P("island", None, "fsdp", None),
        P(),
        P("island", "fsdp", None),
        P("island", None, "fsdp", None),
        P("island", "fsdp", None),
        P("island", "fsdp", None),
        P("fsdp", None),
        P("fsdp", None),
    )
    out_specs = (
        P("island", None, "fsdp", None),
        P("island", "fsdp", None),
        P("fsdp", None),
        P("fsdp", None),
    )
    return jax.shard_map(
        on_device, mesh=mesh, in_specs=in_specs, out_specs=out_specs, check_vma=False
    )
```

```python
import functools
import math

import jax
import jax.numpy as jnp
from jax import lax
from jax.experimental import pallas as pl
from jax.experimental.pallas import tpu as pltpu
from jax.sharding import PartitionSpec as P

BLOCK = 128
NX = 4
NY = 4
NZ = 4
ROWS = 512
KV = 512
D = 8192
HALF = 256
QUARTER = 128
PART = 32
MEET_AFTER = 1
RELAY_AFTER = 4
CHUNK = 64

norm_eps = 1e-05
inner_rate = 0.3
outer_rate = 0.7
keep_rate = 0.9
mix_share = 0.5

MESH = pl.DeviceIdType.MESH
f32 = jnp.float32
bf16 = jnp.bfloat16


def kernel(
    step_scale,
    islands,
    tok_hbm,
    gain_hbm,
    w_hbm,
    cot_hbm,
    lev_hbm,
    scales_hbm,
    ow_hbm,
    mom_hbm,
    keys_out,
    merged_out,
    ow_out,
    mom_out,
    tok,
    gain,
    wf,
    cot,
    lev,
    scales,
    wg,
    acc,
    p_out,
    p_in,
    q,
    r_a,
    r_b,
    from_m,
    from_p,
    z_out,
    z_in,
    y_in,
    zl_out,
    zl_in,
    total_delta,
    load_sem,
    send_sem,
    recv_sem,
    near_sem,
    far_sem,
):
    f = lax.axis_index("fsdp")
    i = lax.axis_index("island")
    zh, x, c = f // 8, (f // 2) % NX, f % 2
    zl, y = i // NY, i % NY

    def fs(dz, dx, dc):
        return ((zh + dz) % 2) * 8 + ((x + dx) % NX) * 2 + (c + dc) % 2

    def to_fsdp(dz, dx, dc):
        return {"fsdp": fs(dz, dx, dc), "island": i}

    def to_island(dzl, dy):
        return {"fsdp": f, "island": ((zl + dzl) % NZ) * NY + (y + dy) % NY}

    right, left = to_fsdp(0, 1, 0), to_fsdp(0, NX - 1, 0)
    across, other = to_fsdp(1, 0, 0), to_fsdp(0, 0, 1)

    started = []
    counter = [0]

    def remote(k, src, dst, device):
        return pltpu.make_async_remote_copy(
            src_ref=src,
            dst_ref=dst,
            send_sem=send_sem.at[k],
            recv_sem=recv_sem.at[k],
            device_id=device,
            device_id_type=MESH,
        )

    def role(src, dst, device):
        copy = remote(counter[0], src, dst, device)
        counter[0] += 1
        started.append(copy)
        return copy

    load_count = [0]

    def load(src, dst):
        copy = pltpu.make_async_copy(src, dst, load_sem.at[load_count[0]])
        load_count[0] += 1
        copy.start()
        return copy

    load_w = []
    for n in range(2):
        rows = pl.ds(n * HALF, HALF)
        load_w.append(load(w_hbm.at[rows], wf.at[rows]))

    barrier = pltpu.get_barrier_semaphore()

    def at_core(device, core):
        return {"fsdp": (device["fsdp"] // 2) * 2 + core, "island": device["island"]}

    near = [right, left]
    far = [across]
    far += [to_island(0, d) for d in (1, 2, 3)] + [to_island(d, 0) for d in (1, 2, 3)]
    pl.semaphore_signal(barrier, inc=1, device_id=other, device_id_type=MESH)
    for core, group in ((0, near), (1, far)):
        for peer in group:
            pl.semaphore_signal(
                barrier, inc=1, device_id=at_core(peer, core), device_id_type=MESH
            )
    load_w[0].wait()
    wg[0, 0, 0, 0:HALF] = wf[0:HALF].astype(bf16)
    load_w[1].wait()
    wg[0, 0, 0, HALF:ROWS] = wf[HALF:ROWS].astype(bf16)

    load_lev = load(lev_hbm, lev)
    load_scales = load(scales_hbm, scales)
    load_gain = load(gain_hbm, gain)
    loads = []
    for n in range(ROWS // CHUNK):
        rows = pl.ds(n * CHUNK, CHUNK)
        loads.append(load(tok_hbm.at[rows], tok.at[rows]))
    load_cot = load(cot_hbm, cot)
    load_ow = load(ow_hbm, ow_out)
    load_mom = load(mom_hbm, mom_out)

    @pl.when(c == 0)
    def _():
        pl.semaphore_wait(barrier, 1 + 2 * len(near))
        pl.semaphore_signal(near_sem, inc=1, device_id=other, device_id_type=MESH)

    @pl.when(c == 1)
    def _():
        pl.semaphore_wait(near_sem, 1)

    def quarter(n):
        return pl.ds(n * QUARTER, QUARTER)

    ag_right, ag_left, ag_relay, ag_other = {}, {}, {}, {}
    for zz in range(2):
        for n in (0, 1, 2, 3):
            rows = quarter(n)
            ag_right[zz, n] = role(wg.at[zz, 0, 0, rows], wg.at[zz, 3, 0, rows], right)
        for n in (1, 0, 3, 2):
            rows = quarter(n)
            ag_left[zz, n] = role(wg.at[zz, 0, 0, rows], wg.at[zz, 1, 0, rows], left)
        for n in (0, 2):
            rows = quarter(n)
            ag_relay[zz, n] = role(wg.at[zz, 3, 0, rows], wg.at[zz, 2, 0, rows], right)
        for n in (1, 3):
            rows = quarter(n)
            ag_relay[zz, n] = role(wg.at[zz, 1, 0, rows], wg.at[zz, 2, 0, rows], left)
        for dx in range(4):
            ag_other[zz, dx] = role(wg.at[zz, dx, 0], wg.at[zz, dx, 1], other)
    ag_z = [role(wg.at[0, 0, 0, quarter(n)], wg.at[1, 0, 0, quarter(n)], across) for n in range(4)]

    low, high = pl.ds(0, HALF), pl.ds(HALF, HALF)
    opp_left, opp_right, dir_right, dir_left, sum_right, sum_left = {}, {}, {}, {}, {}, {}
    for zz in range(2):
        for n in range(2):
            part, upper, lower = quarter(n), quarter(n), quarter(2 + n)
            opp_left[zz, n] = role(q.at[zz, 2, upper], r_a.at[zz, part], left)
            opp_right[zz, n] = role(q.at[zz, 2, lower], r_b.at[zz, part], right)
            sum_left[zz, n] = role(q.at[zz, 3, upper], from_p.at[zz, upper], left)
            sum_right[zz, n] = role(q.at[zz, 1, lower], from_m.at[zz, lower], right)
        dir_right[zz] = role(q.at[zz, 1, low], from_m.at[zz, low], right)
        dir_left[zz] = role(q.at[zz, 3, high], from_p.at[zz, high], left)
    z_send = [role(z_out.at[quarter(n)], z_in.at[quarter(n)], across) for n in range(4)]

    def y_rows(d):
        return pl.ds(pl.multiple_of(((y + d) % NY) * QUARTER, QUARTER), QUARTER)

    def z_rows(d):
        return pl.ds(pl.multiple_of(((zl + d) % NZ) * PART, PART), PART)

    mine = y_rows(0)
    my_part = pl.ds(pl.multiple_of(y * QUARTER + zl * PART, PART), PART)
    steps = (1, 2, 3)
    y_part = [role(lev.at[y_rows(d)], y_in.at[d - 1], to_island(0, d)) for d in steps]
    zl_part = [role(zl_out.at[z_rows(d)], zl_in.at[d - 1], to_island(d, 0)) for d in steps]
    zl_sum = [role(total_delta.at[my_part], total_delta.at[my_part], to_island(d, 0)) for d in steps]
    y_sum = [role(total_delta.at[mine], total_delta.at[mine], to_island(0, d)) for d in steps]

    base = counter[0]

    def pair(zz, dx):
        return remote(base + zz * 4 + dx, p_out.at[zz, dx], p_in.at[zz, dx], other)

    def gather_right_left(zz, n):
        for m in range(2):
            ag_right[zz, 2 * n + m].start()
            ag_left[zz, 2 * n + 1 - m].start()

    gather_right_left(0, 0)
    ag_other[0, 0].start()

    load_lev.wait()
    load_scales.wait()
    by_block = scales[...]
    by_row = jnp.transpose(jnp.concatenate([by_block, by_block], axis=0))
    for b in range(KV // BLOCK):
        cols = pl.ds(b * BLOCK, BLOCK)
        lev[:, cols] = (lev[:, cols].astype(f32) * by_row[:, b : b + 1]).astype(bf16)

    def normalize(first):
        def body(n, carry):
            rows = pl.ds(pl.multiple_of(first + n * 16, 16), 16)
            total = jnp.zeros((16, 128), f32)
            for k in range(D // 128):
                v = tok[rows, k * 128 : (k + 1) * 128].astype(f32)
                total += v * v
            spread = jnp.sum(total, axis=1, keepdims=True) / D
            inv = lax.rsqrt(spread + norm_eps)
            for k in range(D // 128):
                cols = pl.ds(k * 128, 128)
                v = tok[rows, cols].astype(f32)
                tok[rows, cols] = (v * inv * gain[:, cols]).astype(bf16)
            return carry

        lax.fori_loop(0, CHUNK // 16, body, 0)

    def relay(zz, n):
        (ag_right if n % 2 == 0 else ag_left)[zz, n].wait_recv()
        ag_relay[zz, n].start()

    def meet_far():
        @pl.when(c == 1)
        def _():
            pl.semaphore_wait(barrier, 1 + 2 * len(far))
            pl.semaphore_signal(far_sem, inc=1, device_id=other, device_id_type=MESH)

        @pl.when(c == 0)
        def _():
            pl.semaphore_wait(far_sem, 1)

        for n in range(2):
            ag_z[n].start()
        gather_right_left(0, 1)
        for copy in y_part:
            copy.start()

    load_gain.wait()
    for n in range(ROWS // CHUNK):
        loads[n].wait()
        normalize(n * CHUNK)
        if n == MEET_AFTER:
            meet_far()
        if n == RELAY_AFTER:
            relay(0, 0)
            relay(0, 1)
    relay(0, 2)
    relay(0, 3)

    def columns(dz, dx, dc):
        return pl.ds(pl.multiple_of(fs(dz, dx, dc) * ROWS, ROWS), ROWS)

    def gradient(dz, dx, dc):
        return lax.dot_general(
            tok[:, columns(dz, dx, dc)],
            cot[...],
            (((0,), (0,)), ((), ())),
            preferred_element_type=f32,
        )

    def give_gradients(zz):
        def give(n, carry):
            dx = (2 + n) % 4
            p_out[zz, dx] = gradient(zz, dx, 1).astype(bf16)
            pair(zz, dx).start()
            return carry

        lax.fori_loop(0, 4, give, 0)

    def keep_gradients(zz, first, last):
        def keep(n, carry):
            dx = (2 + n) % 4
            pair(zz, dx).wait_recv()
            q[zz, dx] = (gradient(zz, dx, 0) + p_in[zz, dx].astype(f32)).astype(bf16)
            return carry

        lax.fori_loop(first, last, keep, 0)

    def scatter_opposite(zz):
        for n in range(2):
            opp_right[zz, n].start()
            opp_left[zz, n].start()

    def scatter_direct(zz):
        dir_right[zz].start()
        dir_left[zz].start()

    def scatter_sums(zz):
        for n in range(2):
            part, upper, lower = quarter(n), quarter(n), quarter(2 + n)
            opp_right[zz, n].wait_recv()
            q[zz, 1, lower] = (q[zz, 1, lower].astype(f32) + r_b[zz, part].astype(f32)).astype(bf16)
            sum_right[zz, n].start()
            opp_left[zz, n].wait_recv()
            q[zz, 3, upper] = (q[zz, 3, upper].astype(f32) + r_a[zz, part].astype(f32)).astype(bf16)
            sum_left[zz, n].start()

    def key_pair(zz, dx, first=False):
        ag_other[zz, dx].wait_recv()

        def body(dc, carry):
            acc[...] += jnp.dot(
                tok[:, columns(zz, dx, dc)], wg[zz, dx, dc], preferred_element_type=f32
            )
            return carry

        if first:
            acc[...] = jnp.zeros_like(acc)
        lax.fori_loop(0, 2, body, 0)

    def share_neighbours(zz):
        for n in (1, 3):
            ag_right[zz, n].wait_recv()
        ag_other[zz, 3].start()
        for n in (0, 2):
            ag_left[zz, n].wait_recv()
        ag_other[zz, 1].start()

    def share_opposite(zz):
        for n in range(4):
            ag_relay[zz, n].wait_recv()
        ag_other[zz, 2].start()

    load_cot.wait()
    give_gradients(1)

    for copy in y_part:
        copy.wait_recv()
    part = lev[mine].astype(f32)
    for d in range(3):
        part += y_in[d].astype(f32)
    zl_out[...] = part.astype(bf16)
    for copy in zl_part:
        copy.start()

    for n in (2, 3):
        ag_z[n].start()

    keep_gradients(1, 0, 1)
    scatter_opposite(1)
    keep_gradients(1, 1, 4)
    scatter_direct(1)
    share_neighbours(0)

    key_pair(0, 0, first=True)
    give_gradients(0)
    scatter_sums(1)
    share_opposite(0)
    keep_gradients(0, 0, 4)

    key_pair(0, 3)
    key_pair(0, 1)

    dir_right[1].wait_recv()
    dir_left[1].wait_recv()
    for n in range(4):
        ag_z[n].wait_recv()

    def send_across(n):
        rows = quarter(n)
        total = q[1, 0, rows].astype(f32) + from_m[1, rows].astype(f32)
        z_out[rows] = (total + from_p[1, rows].astype(f32)).astype(bf16)
        z_send[n].start()

    sum_left[1, 0].wait_recv()

    gather_right_left(1, 0)
    gather_right_left(1, 1)
    ag_other[1, 0].start()

    for copy in zl_part:
        copy.wait_recv()
    part = zl_out[z_rows(0)].astype(f32)
    for d in range(3):
        part += zl_in[d].astype(f32)
    total_delta[my_part] = part.astype(bf16)
    for copy in zl_sum:
        copy.start()

    send_across(0)
    sum_right[1, 0].wait_recv()
    send_across(2)
    sum_left[1, 1].wait_recv()
    send_across(1)
    sum_right[1, 1].wait_recv()
    send_across(3)

    key_pair(0, 2)
    relay(1, 0)
    relay(1, 1)

    key_pair(1, 0)
    relay(1, 2)
    relay(1, 3)
    scatter_opposite(0)
    scatter_direct(0)
    share_neighbours(1)
    key_pair(1, 3)
    key_pair(1, 1)
    scatter_sums(0)

    for copy in zl_sum:
        copy.wait_recv()
    for copy in y_sum:
        copy.start()

    share_opposite(1)
    key_pair(1, 2)
    keys_out[...] = acc[...].astype(bf16)

    load_ow.wait()
    load_mom.wait()
    for copy in y_sum:
        copy.wait_recv()

    def outer(n, carry):
        rows = pl.ds(pl.multiple_of(n * PART, PART), PART)
        mean = total_delta[rows].astype(f32) / islands
        momentum = keep_rate * mom_out[rows] + mean
        mom_out[rows] = momentum
        ow_out[rows] = ow_out[rows] - outer_rate * (mean + keep_rate * momentum)
        return carry

    lax.fori_loop(0, ROWS // PART, outer, 0)

    for n in range(4):
        z_send[n].wait_recv()
    dir_right[0].wait_recv()
    dir_left[0].wait_recv()

    def finish(n):
        rows = quarter(n)
        total = q[0, 0, rows].astype(f32) + z_in[rows].astype(f32)
        total += from_m[0, rows].astype(f32) + from_p[0, rows].astype(f32)
        inner = wf[rows] - step_scale * total
        merged_out[rows] = mix_share * inner + (1.0 - mix_share) * ow_out[rows]

    for n in range(2):
        sum_left[0, n].wait_recv()
        finish(n)
        sum_right[0, n].wait_recv()
        finish(2 + n)
    for copy in started:
        copy.wait_send()

    def drain(n, carry):
        pair(n // 4, n % 4).wait_send()
        return carry

    lax.fori_loop(0, 8, drain, 0)


def write(keys, merged, weights, momentum, keys_hbm, merged_hbm, weights_hbm, momentum_hbm, sem):
    pairs = ((merged, merged_hbm), (weights, weights_hbm), (momentum, momentum_hbm), (keys, keys_hbm))
    copies = [pltpu.make_async_copy(a, b, sem.at[n]) for n, (a, b) in enumerate(pairs)]
    for copy in copies:
        copy.start()
    for copy in copies:
        copy.wait()


N_ROLES = 160


def on_device(
    tokens_in,
    norm_gain,
    local_weights,
    cotangent,
    delta_levels,
    block_scales,
    outer_weights_in,
    momentum_in,
):
    features = tokens_in.shape[-1]
    groups = lax.axis_size("fsdp")
    islands = lax.axis_size("island")
    tokens = tokens_in[0].reshape(-1, features)
    tangent = cotangent[0].reshape(-1, cotangent.shape[-1])
    local_rows = tokens.shape[0]
    step_scale = inner_rate / math.sqrt(features) / math.sqrt(local_rows * groups)

    hbm = pl.BlockSpec(memory_space=pltpu.HBM)
    vmem = pl.BlockSpec(memory_space=pltpu.VMEM)
    shapes = (
        jax.ShapeDtypeStruct((ROWS, KV), bf16),
        jax.ShapeDtypeStruct((ROWS, KV), f32),
        jax.ShapeDtypeStruct((ROWS, KV), f32),
        jax.ShapeDtypeStruct((ROWS, KV), f32),
    )
    results = pl.pallas_call(
        functools.partial(kernel, step_scale, islands),
        out_shape=tuple(pltpu.VMEM(s.shape, s.dtype) for s in shapes),
        in_specs=[hbm] * 8,
        out_specs=(vmem,) * 4,
        scratch_shapes=[
            pltpu.VMEM((ROWS, D), bf16),
            pltpu.VMEM((1, D), f32),
            pltpu.VMEM((ROWS, KV), f32),
            pltpu.VMEM((ROWS, KV), bf16),
            pltpu.VMEM((ROWS, KV), bf16),
            pltpu.VMEM((KV // BLOCK, ROWS), f32),
            pltpu.VMEM((2, 4, 2, ROWS, KV), bf16),
            pltpu.VMEM((ROWS, KV), f32),
            pltpu.VMEM((2, 4, ROWS, KV), bf16),
            pltpu.VMEM((2, 4, ROWS, KV), bf16),
            pltpu.VMEM((2, 4, ROWS, KV), bf16),
            pltpu.VMEM((2, HALF, KV), bf16),
            pltpu.VMEM((2, HALF, KV), bf16),
            pltpu.VMEM((2, ROWS, KV), bf16),
            pltpu.VMEM((2, ROWS, KV), bf16),
            pltpu.VMEM((ROWS, KV), bf16),
            pltpu.VMEM((ROWS, KV), bf16),
            pltpu.VMEM((3, QUARTER, KV), bf16),
            pltpu.VMEM((QUARTER, KV), bf16),
            pltpu.VMEM((3, PART, KV), bf16),
            pltpu.VMEM((ROWS, KV), bf16),
            pltpu.SemaphoreType.DMA((8 + ROWS // CHUNK,)),
            pltpu.SemaphoreType.DMA((N_ROLES,)),
            pltpu.SemaphoreType.DMA((N_ROLES,)),
            pltpu.SemaphoreType.REGULAR,
            pltpu.SemaphoreType.REGULAR,
        ],
        compiler_params=pltpu.CompilerParams(
            collective_id=0, has_side_effects=True, vmem_limit_bytes=56 * 2**20
        ),
        cost_estimate=pl.CostEstimate(
            flops=4 * ROWS * D * KV, bytes_accessed=14 * 2**20, transcendentals=ROWS
        ),
    )(
        tokens,
        norm_gain.reshape(1, -1),
        local_weights[0],
        tangent,
        delta_levels[0],
        block_scales[0].T,
        outer_weights_in,
        momentum_in,
    )
    keys, merged, weights_new, momentum_new = pl.pallas_call(
        write,
        out_shape=shapes,
        in_specs=[vmem] * 4,
        out_specs=(hbm,) * 4,
        scratch_shapes=[pltpu.SemaphoreType.DMA((4,))],
        compiler_params=pltpu.CompilerParams(vmem_limit_bytes=2**20),
    )(*results)
    return (keys.reshape(cotangent.shape), merged[None], weights_new, momentum_new)


def solution(mesh):
    in_specs = (
        P("island", None, "fsdp", None),
        P(),
        P("island", "fsdp", None),
        P("island", None, "fsdp", None),
        P("island", "fsdp", None),
        P("island", "fsdp", None),
        P("fsdp", None),
        P("fsdp", None),
    )
    out_specs = (
        P("island", None, "fsdp", None),
        P("island", "fsdp", None),
        P("fsdp", None),
        P("fsdp", None),
    )
    return jax.shard_map(
        on_device, mesh=mesh, in_specs=in_specs, out_specs=out_specs, check_vma=False
    )
```

```python
import functools
import math

import jax
import jax.numpy as jnp
from jax import lax
from jax.experimental import pallas as pl
from jax.experimental.pallas import tpu as pltpu
from jax.sharding import PartitionSpec as P

BLOCK = 128
NX = 4
NY = 4
NZ = 4
ROWS = 512
KV = 512
D = 8192
HALF = 256
QUARTER = 128
PART = 32
MEET_AFTER = 1
RELAY_AFTER = 4
CHUNK = 64

norm_eps = 1e-05
inner_rate = 0.3
outer_rate = 0.7
keep_rate = 0.9
mix_share = 0.5

MESH = pl.DeviceIdType.MESH
f32 = jnp.float32
bf16 = jnp.bfloat16


def kernel(
    step_scale,
    islands,
    tok_hbm,
    gain_hbm,
    w_hbm,
    cot_hbm,
    lev_hbm,
    scales_hbm,
    ow_hbm,
    mom_hbm,
    keys_out,
    merged_out,
    ow_out,
    mom_out,
    tok,
    gain,
    wf,
    cot,
    lev,
    scales,
    wg,
    acc,
    p_out,
    p_in,
    q,
    r_a,
    r_b,
    from_m,
    from_p,
    z_out,
    z_in,
    y_in,
    zl_out,
    zl_in,
    total_delta,
    load_sem,
    send_sem,
    recv_sem,
    near_sem,
    far_sem,
):
    f = lax.axis_index("fsdp")
    i = lax.axis_index("island")
    zh, x, c = f // 8, (f // 2) % NX, f % 2
    zl, y = i // NY, i % NY

    def fs(dz, dx, dc):
        return ((zh + dz) % 2) * 8 + ((x + dx) % NX) * 2 + (c + dc) % 2

    def to_fsdp(dz, dx, dc):
        return {"fsdp": fs(dz, dx, dc), "island": i}

    def to_island(dzl, dy):
        return {"fsdp": f, "island": ((zl + dzl) % NZ) * NY + (y + dy) % NY}

    right, left = to_fsdp(0, 1, 0), to_fsdp(0, NX - 1, 0)
    across, other = to_fsdp(1, 0, 0), to_fsdp(0, 0, 1)

    started = []
    counter = [0]

    def remote(k, src, dst, device):
        return pltpu.make_async_remote_copy(
            src_ref=src,
            dst_ref=dst,
            send_sem=send_sem.at[k],
            recv_sem=recv_sem.at[k],
            device_id=device,
            device_id_type=MESH,
        )

    def role(src, dst, device):
        copy = remote(counter[0], src, dst, device)
        counter[0] += 1
        started.append(copy)
        return copy

    load_count = [0]

    def load(src, dst):
        copy = pltpu.make_async_copy(src, dst, load_sem.at[load_count[0]])
        load_count[0] += 1
        copy.start()
        return copy

    load_w = []
    for n in range(2):
        rows = pl.ds(n * HALF, HALF)
        load_w.append(load(w_hbm.at[rows], wf.at[rows]))

    barrier = pltpu.get_barrier_semaphore()

    def at_core(device, core):
        return {"fsdp": (device["fsdp"] // 2) * 2 + core, "island": device["island"]}

    near = [right, left]
    far = [across]
    far += [to_island(0, d) for d in (1, 2, 3)] + [to_island(d, 0) for d in (1, 2, 3)]
    pl.semaphore_signal(barrier, inc=1, device_id=other, device_id_type=MESH)
    for core, group in ((0, near), (1, far)):
        for peer in group:
            pl.semaphore_signal(
                barrier, inc=1, device_id=at_core(peer, core), device_id_type=MESH
            )
    load_w[0].wait()
    wg[0, 0, 0, 0:HALF] = wf[0:HALF].astype(bf16)
    load_w[1].wait()
    wg[0, 0, 0, HALF:ROWS] = wf[HALF:ROWS].astype(bf16)

    load_lev = load(lev_hbm, lev)
    load_scales = load(scales_hbm, scales)
    load_gain = load(gain_hbm, gain)
    loads = []
    for n in range(ROWS // CHUNK):
        rows = pl.ds(n * CHUNK, CHUNK)
        loads.append(load(tok_hbm.at[rows], tok.at[rows]))
    load_cot = load(cot_hbm, cot)
    load_ow = load(ow_hbm, ow_out)
    load_mom = load(mom_hbm, mom_out)

    @pl.when(c == 0)
    def _():
        pl.semaphore_wait(barrier, 1 + 2 * len(near))
        pl.semaphore_signal(near_sem, inc=1, device_id=other, device_id_type=MESH)

    @pl.when(c == 1)
    def _():
        pl.semaphore_wait(near_sem, 1)

    def quarter(n):
        return pl.ds(n * QUARTER, QUARTER)

    ag_right, ag_left, ag_relay, ag_other = {}, {}, {}, {}
    for zz in range(2):
        for n in (0, 1, 2, 3):
            rows = quarter(n)
            ag_right[zz, n] = role(wg.at[zz, 0, 0, rows], wg.at[zz, 3, 0, rows], right)
        for n in (1, 0, 3, 2):
            rows = quarter(n)
            ag_left[zz, n] = role(wg.at[zz, 0, 0, rows], wg.at[zz, 1, 0, rows], left)
        for n in (0, 2):
            rows = quarter(n)
            ag_relay[zz, n] = role(wg.at[zz, 3, 0, rows], wg.at[zz, 2, 0, rows], right)
        for n in (1, 3):
            rows = quarter(n)
            ag_relay[zz, n] = role(wg.at[zz, 1, 0, rows], wg.at[zz, 2, 0, rows], left)
        for dx in range(4):
            ag_other[zz, dx] = role(wg.at[zz, dx, 0], wg.at[zz, dx, 1], other)
    ag_z = [role(wg.at[0, 0, 0, quarter(n)], wg.at[1, 0, 0, quarter(n)], across) for n in range(4)]

    low, high = pl.ds(0, HALF), pl.ds(HALF, HALF)
    opp_left, opp_right, dir_right, dir_left, sum_right, sum_left = {}, {}, {}, {}, {}, {}
    for zz in range(2):
        for n in range(2):
            part, upper, lower = quarter(n), quarter(n), quarter(2 + n)
            opp_left[zz, n] = role(q.at[zz, 2, upper], r_a.at[zz, part], left)
            opp_right[zz, n] = role(q.at[zz, 2, lower], r_b.at[zz, part], right)
            sum_left[zz, n] = role(q.at[zz, 3, upper], from_p.at[zz, upper], left)
            sum_right[zz, n] = role(q.at[zz, 1, lower], from_m.at[zz, lower], right)
        dir_right[zz] = role(q.at[zz, 1, low], from_m.at[zz, low], right)
        dir_left[zz] = role(q.at[zz, 3, high], from_p.at[zz, high], left)
    z_send = [role(z_out.at[quarter(n)], z_in.at[quarter(n)], across) for n in range(4)]

    def y_rows(d):
        return pl.ds(pl.multiple_of(((y + d) % NY) * QUARTER, QUARTER), QUARTER)

    def z_rows(d):
        return pl.ds(pl.multiple_of(((zl + d) % NZ) * PART, PART), PART)

    mine = y_rows(0)
    my_part = pl.ds(pl.multiple_of(y * QUARTER + zl * PART, PART), PART)
    steps = (1, 2, 3)
    y_part = [role(lev.at[y_rows(d)], y_in.at[d - 1], to_island(0, d)) for d in steps]
    zl_part = [role(zl_out.at[z_rows(d)], zl_in.at[d - 1], to_island(d, 0)) for d in steps]
    zl_sum = [role(total_delta.at[my_part], total_delta.at[my_part], to_island(d, 0)) for d in steps]
    y_sum = [role(total_delta.at[mine], total_delta.at[mine], to_island(0, d)) for d in steps]

    base = counter[0]

    def pair(zz, dx):
        return remote(base + zz * 4 + dx, p_out.at[zz, dx], p_in.at[zz, dx], other)

    def gather_right_left(zz, n):
        for m in range(2):
            ag_right[zz, 2 * n + m].start()
            ag_left[zz, 2 * n + 1 - m].start()

    gather_right_left(0, 0)
    ag_other[0, 0].start()

    load_lev.wait()
    load_scales.wait()
    by_block = scales[...]
    by_row = jnp.transpose(jnp.concatenate([by_block, by_block], axis=0))
    for b in range(KV // BLOCK):
        cols = pl.ds(b * BLOCK, BLOCK)
        lev[:, cols] = (lev[:, cols].astype(f32) * by_row[:, b : b + 1]).astype(bf16)

    def normalize(first):
        def body(n, carry):
            rows = pl.ds(pl.multiple_of(first + n * 16, 16), 16)
            total = jnp.zeros((16, 128), f32)
            for k in range(D // 128):
                v = tok[rows, k * 128 : (k + 1) * 128].astype(f32)
                total += v * v
            spread = jnp.sum(total, axis=1, keepdims=True) / D
            inv = lax.rsqrt(spread + norm_eps)
            for k in range(D // 128):
                cols = pl.ds(k * 128, 128)
                v = tok[rows, cols].astype(f32)
                tok[rows, cols] = (v * inv * gain[:, cols]).astype(bf16)
            return carry

        lax.fori_loop(0, CHUNK // 16, body, 0)

    def relay(zz, n):
        (ag_right if n % 2 == 0 else ag_left)[zz, n].wait_recv()
        ag_relay[zz, n].start()

    def meet_far():
        @pl.when(c == 1)
        def _():
            pl.semaphore_wait(barrier, 1 + 2 * len(far))
            pl.semaphore_signal(far_sem, inc=1, device_id=other, device_id_type=MESH)

        @pl.when(c == 0)
        def _():
            pl.semaphore_wait(far_sem, 1)

        for n in range(2):
            ag_z[n].start()
        gather_right_left(0, 1)
        for copy in y_part:
            copy.start()

    load_gain.wait()
    for n in range(ROWS // CHUNK):
        loads[n].wait()
        normalize(n * CHUNK)
        if n == MEET_AFTER:
            meet_far()
        if n == RELAY_AFTER:
            relay(0, 0)
            relay(0, 1)
    relay(0, 2)
    relay(0, 3)

    def columns(dz, dx, dc):
        return pl.ds(pl.multiple_of(fs(dz, dx, dc) * ROWS, ROWS), ROWS)

    def gradient(dz, dx, dc):
        return lax.dot_general(
            tok[:, columns(dz, dx, dc)],
            cot[...],
            (((0,), (0,)), ((), ())),
            preferred_element_type=f32,
        )

    def give_gradients(zz):
        def give(n, carry):
            dx = (2 + n) % 4
            p_out[zz, dx] = gradient(zz, dx, 1).astype(bf16)
            pair(zz, dx).start()
            return carry

        lax.fori_loop(0, 4, give, 0)

    def keep_gradients(zz, first, last):
        def keep(n, carry):
            dx = (2 + n) % 4
            pair(zz, dx).wait_recv()
            q[zz, dx] = (gradient(zz, dx, 0) + p_in[zz, dx].astype(f32)).astype(bf16)
            return carry

        lax.fori_loop(first, last, keep, 0)

    def scatter_opposite(zz):
        for n in range(2):
            opp_right[zz, n].start()
            opp_left[zz, n].start()

    def scatter_direct(zz):
        dir_right[zz].start()
        dir_left[zz].start()

    def scatter_sums(zz):
        for n in range(2):
            part, upper, lower = quarter(n), quarter(n), quarter(2 + n)
            opp_right[zz, n].wait_recv()
            q[zz, 1, lower] = (q[zz, 1, lower].astype(f32) + r_b[zz, part].astype(f32)).astype(bf16)
            sum_right[zz, n].start()
            opp_left[zz, n].wait_recv()
            q[zz, 3, upper] = (q[zz, 3, upper].astype(f32) + r_a[zz, part].astype(f32)).astype(bf16)
            sum_left[zz, n].start()

    def key_pair(zz, dx, first=False):
        ag_other[zz, dx].wait_recv()

        def body(dc, carry):
            acc[...] += jnp.dot(
                tok[:, columns(zz, dx, dc)], wg[zz, dx, dc], preferred_element_type=f32
            )
            return carry

        if first:
            acc[...] = jnp.zeros_like(acc)
        lax.fori_loop(0, 2, body, 0)

    def share_neighbours(zz):
        for n in (1, 3):
            ag_right[zz, n].wait_recv()
        ag_other[zz, 3].start()
        for n in (0, 2):
            ag_left[zz, n].wait_recv()
        ag_other[zz, 1].start()

    def share_opposite(zz):
        for n in range(4):
            ag_relay[zz, n].wait_recv()
        ag_other[zz, 2].start()

    load_cot.wait()
    give_gradients(1)

    for n in (2, 3):
        ag_z[n].start()

    keep_gradients(1, 0, 1)
    scatter_opposite(1)
    keep_gradients(1, 1, 4)
    scatter_direct(1)

    for copy in y_part:
        copy.wait_recv()
    part = lev[mine].astype(f32)
    for d in range(3):
        part += y_in[d].astype(f32)
    zl_out[...] = part.astype(bf16)
    for copy in zl_part:
        copy.start()
    share_neighbours(0)

    key_pair(0, 0, first=True)
    give_gradients(0)
    scatter_sums(1)
    share_opposite(0)
    keep_gradients(0, 0, 4)

    key_pair(0, 3)
    key_pair(0, 1)

    dir_right[1].wait_recv()
    dir_left[1].wait_recv()
    for n in range(4):
        ag_z[n].wait_recv()

    def send_across(n):
        rows = quarter(n)
        total = q[1, 0, rows].astype(f32) + from_m[1, rows].astype(f32)
        z_out[rows] = (total + from_p[1, rows].astype(f32)).astype(bf16)
        z_send[n].start()

    sum_left[1, 0].wait_recv()

    gather_right_left(1, 0)
    gather_right_left(1, 1)
    ag_other[1, 0].start()

    for copy in zl_part:
        copy.wait_recv()
    part = zl_out[z_rows(0)].astype(f32)
    for d in range(3):
        part += zl_in[d].astype(f32)
    total_delta[my_part] = part.astype(bf16)
    for copy in zl_sum:
        copy.start()

    send_across(0)
    sum_right[1, 0].wait_recv()
    send_across(2)
    sum_left[1, 1].wait_recv()
    send_across(1)
    sum_right[1, 1].wait_recv()
    send_across(3)

    key_pair(0, 2)
    relay(1, 0)
    relay(1, 1)

    key_pair(1, 0)
    relay(1, 2)
    relay(1, 3)
    scatter_opposite(0)
    scatter_direct(0)
    share_neighbours(1)
    key_pair(1, 3)
    key_pair(1, 1)
    scatter_sums(0)

    for copy in zl_sum:
        copy.wait_recv()
    for copy in y_sum:
        copy.start()

    share_opposite(1)
    key_pair(1, 2)
    keys_out[...] = acc[...].astype(bf16)

    load_ow.wait()
    load_mom.wait()
    for copy in y_sum:
        copy.wait_recv()

    def outer(n, carry):
        rows = pl.ds(pl.multiple_of(n * PART, PART), PART)
        mean = total_delta[rows].astype(f32) / islands
        momentum = keep_rate * mom_out[rows] + mean
        mom_out[rows] = momentum
        ow_out[rows] = ow_out[rows] - outer_rate * (mean + keep_rate * momentum)
        return carry

    lax.fori_loop(0, ROWS // PART, outer, 0)

    for n in range(4):
        z_send[n].wait_recv()
    dir_right[0].wait_recv()
    dir_left[0].wait_recv()

    def finish(n):
        rows = quarter(n)
        total = q[0, 0, rows].astype(f32) + z_in[rows].astype(f32)
        total += from_m[0, rows].astype(f32) + from_p[0, rows].astype(f32)
        inner = wf[rows] - step_scale * total
        merged_out[rows] = mix_share * inner + (1.0 - mix_share) * ow_out[rows]

    for n in range(2):
        sum_left[0, n].wait_recv()
        finish(n)
        sum_right[0, n].wait_recv()
        finish(2 + n)
    for copy in started:
        copy.wait_send()

    def drain(n, carry):
        pair(n // 4, n % 4).wait_send()
        return carry

    lax.fori_loop(0, 8, drain, 0)


def write(keys, merged, weights, momentum, keys_hbm, merged_hbm, weights_hbm, momentum_hbm, sem):
    pairs = ((merged, merged_hbm), (weights, weights_hbm), (momentum, momentum_hbm), (keys, keys_hbm))
    copies = [pltpu.make_async_copy(a, b, sem.at[n]) for n, (a, b) in enumerate(pairs)]
    for copy in copies:
        copy.start()
    for copy in copies:
        copy.wait()


N_ROLES = 160


def on_device(
    tokens_in,
    norm_gain,
    local_weights,
    cotangent,
    delta_levels,
    block_scales,
    outer_weights_in,
    momentum_in,
):
    features = tokens_in.shape[-1]
    groups = lax.axis_size("fsdp")
    islands = lax.axis_size("island")
    tokens = tokens_in[0].reshape(-1, features)
    tangent = cotangent[0].reshape(-1, cotangent.shape[-1])
    local_rows = tokens.shape[0]
    step_scale = inner_rate / math.sqrt(features) / math.sqrt(local_rows * groups)

    hbm = pl.BlockSpec(memory_space=pltpu.HBM)
    vmem = pl.BlockSpec(memory_space=pltpu.VMEM)
    shapes = (
        jax.ShapeDtypeStruct((ROWS, KV), bf16),
        jax.ShapeDtypeStruct((ROWS, KV), f32),
        jax.ShapeDtypeStruct((ROWS, KV), f32),
        jax.ShapeDtypeStruct((ROWS, KV), f32),
    )
    results = pl.pallas_call(
        functools.partial(kernel, step_scale, islands),
        out_shape=tuple(pltpu.VMEM(s.shape, s.dtype) for s in shapes),
        in_specs=[hbm] * 8,
        out_specs=(vmem,) * 4,
        scratch_shapes=[
            pltpu.VMEM((ROWS, D), bf16),
            pltpu.VMEM((1, D), f32),
            pltpu.VMEM((ROWS, KV), f32),
            pltpu.VMEM((ROWS, KV), bf16),
            pltpu.VMEM((ROWS, KV), bf16),
            pltpu.VMEM((KV // BLOCK, ROWS), f32),
            pltpu.VMEM((2, 4, 2, ROWS, KV), bf16),
            pltpu.VMEM((ROWS, KV), f32),
            pltpu.VMEM((2, 4, ROWS, KV), bf16),
            pltpu.VMEM((2, 4, ROWS, KV), bf16),
            pltpu.VMEM((2, 4, ROWS, KV), bf16),
            pltpu.VMEM((2, HALF, KV), bf16),
            pltpu.VMEM((2, HALF, KV), bf16),
            pltpu.VMEM((2, ROWS, KV), bf16),
            pltpu.VMEM((2, ROWS, KV), bf16),
            pltpu.VMEM((ROWS, KV), bf16),
            pltpu.VMEM((ROWS, KV), bf16),
            pltpu.VMEM((3, QUARTER, KV), bf16),
            pltpu.VMEM((QUARTER, KV), bf16),
            pltpu.VMEM((3, PART, KV), bf16),
            pltpu.VMEM((ROWS, KV), bf16),
            pltpu.SemaphoreType.DMA((8 + ROWS // CHUNK,)),
            pltpu.SemaphoreType.DMA((N_ROLES,)),
            pltpu.SemaphoreType.DMA((N_ROLES,)),
            pltpu.SemaphoreType.REGULAR,
            pltpu.SemaphoreType.REGULAR,
        ],
        compiler_params=pltpu.CompilerParams(
            collective_id=0, has_side_effects=True, vmem_limit_bytes=56 * 2**20
        ),
        cost_estimate=pl.CostEstimate(
            flops=4 * ROWS * D * KV, bytes_accessed=14 * 2**20, transcendentals=ROWS
        ),
    )(
        tokens,
        norm_gain.reshape(1, -1),
        local_weights[0],
        tangent,
        delta_levels[0],
        block_scales[0].T,
        outer_weights_in,
        momentum_in,
    )
    keys, merged, weights_new, momentum_new = pl.pallas_call(
        write,
        out_shape=shapes,
        in_specs=[vmem] * 4,
        out_specs=(hbm,) * 4,
        scratch_shapes=[pltpu.SemaphoreType.DMA((4,))],
        compiler_params=pltpu.CompilerParams(vmem_limit_bytes=2**20),
    )(*results)
    return (keys.reshape(cotangent.shape), merged[None], weights_new, momentum_new)


def solution(mesh):
    in_specs = (
        P("island", None, "fsdp", None),
        P(),
        P("island", "fsdp", None),
        P("island", None, "fsdp", None),
        P("island", "fsdp", None),
        P("island", "fsdp", None),
        P("fsdp", None),
        P("fsdp", None),
    )
    out_specs = (
        P("island", None, "fsdp", None),
        P("island", "fsdp", None),
        P("fsdp", None),
        P("fsdp", None),
    )
    return jax.shard_map(
        on_device, mesh=mesh, in_specs=in_specs, out_specs=out_specs, check_vma=False
    )
```
